768 devices in a mesh: gz: 192 (over x, y_hi, z, core), xy: 4 (over y_lo).
Axes of the slice: x: 4, y: 8 (y_hi: 2, y_lo: 4; y = y_hi * 4 + y_lo), z: 12, core: 2. Of those that a mesh axis runs over, the one named last changes fastest.
Arguments:
- coords: float32 [3, 384, 8, 128], P(None, 'gz', 'xy'), may hold values from 0 to 1
- species: int32 [384, 8, 128], P('gz', 'xy'), may hold values from 0 to 7
- centers: int32 [384, 8, 128], P('gz', 'xy'), may hold values from 0 to 127
- others: int32 [384, 8, 128], P('gz', 'xy'), may hold values from 0 to 1151
- live_count: int32 [384, 8], P('gz', 'xy'), may hold values from 42 to 128
- in_weight: float32 [24, 128], replicated, may hold values from -1.25 to 1.25
- env_weight: float32 [128, 32], replicated, may hold values from -0.5 to 0.5
- up_weight: float32 [160, 128], replicated, may hold values from -0.5 to 0.5
- out_weight: float32 [128], replicated, may hold values from -0.5 to 0.5
Outputs:
- atom_energy: float32 [384, 8, 128], P('gz', 'xy')
- forces: float32 [3, 384, 8, 128], P(None, 'gz', 'xy')
The draws below stay inside these ranges and needn't reach their ends.
Inputs may be any that keep to these rules, and one draw needn't show every extreme that they name: Edge slots at or after live_count of a bin are padding; at most 128 are live.
All inputs are finite; a program needn't handle non-finite values.
Results may differ from the reference program's by a relative error of at most 0.0018.
Values may be sent and summed in bfloat16 or wider, within the bound.
No kernel may reach another device: no remote copies, remote signals or barrier semaphores. Data moves between devices by JAX's collectives and lax.ppermute only.
A program may use at most 32 MiB of HBM per device.

```python
import jax
import jax.numpy as jnp
from jax import lax

BIN = 128
NB = 8
SPEC = 8
LAT = 128
CH = 32
EDGES = 128
NBZ = 384
NBX = 8


def touch_ends(array, own_key, least, largest):
    longest = array.shape.index(max(array.shape))
    spots = []
    for shift in (0, 1):
        where = [jax.random.randint(jax.random.fold_in(own_key, axis), (), 0, length) for axis, length in enumerate(array.shape)]
        where[longest] = (where[longest] + shift) % array.shape[longest]
        spots.append(tuple(where))
    return array.at[spots[0]].set(least).at[spots[1]].set(largest)


def levels(rng, shape, cuts, smallest, high):
    gain, own = 1.0, jax.random.fold_in(rng, 6)
    for axis_at, shards_of in cuts:
        steps = jnp.exp(jax.random.uniform(jax.random.fold_in(own, axis_at), (shards_of,), jnp.float32, smallest / len(cuts), high / len(cuts)))
        gain = gain * jnp.repeat(steps, shape[axis_at] // shards_of).reshape([-1 if axis == axis_at else 1 for axis in range(len(shape))])
    return gain


def scatter_about(key, extent, spread, reach, kind=jnp.bfloat16):
    return jnp.clip(spread * jax.random.normal(key, extent, jnp.float32), -reach, reach).astype(kind)


def setup_inputs(seed: int = 0) -> dict:
    arg_keys = jax.random.split(jax.random.key(seed), 10)
    return {
        "coords": jnp.clip(1.0 * jax.random.uniform(arg_keys[0], (3, NBZ, NBX, BIN), jnp.float32) ** levels(arg_keys[0], (3, NBZ, NBX, BIN), ((1, 192), (2, 4)), -0.2, 0.2), 0.0, 1.0),
        "species": touch_ends(jax.random.randint(arg_keys[1], (NBZ, NBX, BIN), 0, SPEC), jax.random.fold_in(arg_keys[1], 1), 0, SPEC - 1).astype(jnp.int32),
        "centers": touch_ends(jax.random.randint(arg_keys[2], (NBZ, NBX, EDGES), 0, BIN), jax.random.fold_in(arg_keys[2], 1), 0, BIN - 1).astype(jnp.int32),
        "others": touch_ends(jax.random.randint(arg_keys[3], (NBZ, NBX, EDGES), 0, 9 * BIN), jax.random.fold_in(arg_keys[3], 1), 0, (9 * BIN) - 1).astype(jnp.int32),
        "live_count": touch_ends(jax.random.randint(arg_keys[4], (NBZ, NBX), EDGES // 3, EDGES + 1), jax.random.fold_in(arg_keys[4], 1), EDGES // 3, EDGES).astype(jnp.int32),
        "in_weight": scatter_about(arg_keys[5], (NB + 2 * SPEC, LAT), (NB + 2 * SPEC) ** -0.5, 1.25, jnp.float32),
        "env_weight": scatter_about(arg_keys[6], (LAT, CH), LAT ** -0.5, 0.5, jnp.float32),
        "up_weight": scatter_about(arg_keys[7], (LAT + CH, LAT), (LAT + CH) ** -0.5, 0.5, jnp.float32),
        "out_weight": scatter_about(arg_keys[8], (LAT,), LAT ** -0.5, 0.5, jnp.float32),
    }


SOFTEN = 0.01
CUTOFF = 3.5
HIGH = lax.Precision.HIGHEST

def neighbourhood(lattice):
    depth_bins = lattice.shape[-3] - 2
    span_bins = lattice.shape[-2] - 2
    blocks = []
    for offset in range(9):
        start_z = offset // 3
        start_x = offset % 3
        blocks.append(lattice[..., start_z:start_z + depth_bins, start_x:start_x + span_bins, :])
    return jnp.concatenate(blocks, axis=-1)

def pick(lattice, indices):
    return jnp.take_along_axis(lattice, jnp.broadcast_to(indices, lattice.shape[:1] + indices.shape), axis=-1)

def live_mask(live_count, edge_count):
    return (jnp.arange(edge_count)[None, None, :] < live_count[..., None]).astype(jnp.float32)

def geometry(coord_ext, spec_ext, centers, others, in_weight):
    interior = coord_ext[:, 1:-1, 1:-1]
    at_center = pick(interior, centers)
    at_other = pick(neighbourhood(coord_ext), others)
    placement = others // 128
    shift_z = (placement // 3 - 1).astype(jnp.float32)
    shift_x = (placement % 3 - 1).astype(jnp.float32)
    along_z = shift_z + at_other[0] - at_center[0]
    across = shift_x + at_other[1] - at_center[1]
    along_y = at_other[2] - at_center[2]
    distance = jnp.sqrt(along_z * along_z + across * across + along_y * along_y + SOFTEN)
    scaled = distance / CUTOFF
    envelope = (1.0 - scaled * scaled) ** 2
    orders = jnp.arange(1, NB + 1).astype(jnp.float32)[:, None, None, None]
    radial = jnp.sin(orders * jnp.pi * scaled[None]) / distance[None] * envelope[None]
    species_ids = jnp.arange(SPEC).astype(spec_ext.dtype)[:, None, None, None]
    spec_center = pick(spec_ext[None, 1:-1, 1:-1], centers)
    spec_other = pick(neighbourhood(spec_ext[None]), others)
    inputs = jnp.concatenate([radial, (spec_center == species_ids).astype(jnp.float32), (spec_other == species_ids).astype(jnp.float32)], axis=0)
    latent = jax.nn.silu(jnp.einsum('kabe,kl->labe', inputs, in_weight, precision=HIGH))
    harmonics = jnp.stack([jnp.ones_like(distance), along_z / distance, across / distance, along_y / distance])
    return (latent, harmonics, envelope)

def features(latent, harmonics, centers, live_count, env_weight):
    edge_count = centers.shape[-1]
    weights = jnp.einsum('labe,lc->cabe', latent, env_weight, precision=HIGH) * live_mask(live_count, edge_count)[None]
    messages = (weights[:, None] * harmonics[None]).reshape((-1,) + centers.shape)
    one_hot = (centers[..., None] == jnp.arange(128)).astype(jnp.float32)
    return jnp.einsum('fabe,aben->fabn', messages, one_hot, precision=HIGH) * (128.0 / edge_count)

def energy(latent, envelope, feature_ext, centers, others, live_count, up_weight, out_weight):
    channels = feature_ext.shape[0] // 4
    feat_center = pick(feature_ext[:, 1:-1, 1:-1], centers)
    feat_other = pick(neighbourhood(feature_ext), others)
    products = (feat_center * feat_other).reshape((channels, 4) + centers.shape).sum(axis=1)
    joined = jnp.concatenate([latent, products], axis=0)
    hidden = jax.nn.silu(jnp.einsum('kabe,kl->labe', joined, up_weight, precision=HIGH))
    edge_energy = jnp.einsum('labe,l->abe', hidden, out_weight, precision=HIGH) * envelope * live_mask(live_count, centers.shape[-1])
    one_hot = (centers[..., None] == jnp.arange(128)).astype(jnp.float32)
    atom_energy = jnp.einsum('abe,aben->abn', edge_energy, one_hot, precision=HIGH)
    return (jnp.sum(edge_energy), atom_energy)

def wrap_pad(lattice, first_dim):
    widths = [(0, 0)] * lattice.ndim
    widths[first_dim] = (1, 1)
    widths[first_dim + 1] = (1, 1)
    return jnp.pad(lattice, widths, mode='wrap')

def reference(coords, species, centers, others, live_count, in_weight, env_weight, up_weight, out_weight):
    row_count = coords.shape[1]
    spec_pad = wrap_pad(species, 0)
    row_ids = jnp.arange(row_count).astype(jnp.int32)

    def total(coords_now):
        coord_pad = wrap_pad(coords_now, 1)

        def row_latent(row_index):
            coord_block = lax.dynamic_slice_in_dim(coord_pad, row_index, 3, 1)
            spec_block = lax.dynamic_slice_in_dim(spec_pad, row_index, 3, 0)
            center_row = lax.dynamic_slice_in_dim(centers, row_index, 1, 0)
            other_row = lax.dynamic_slice_in_dim(others, row_index, 1, 0)
            live_row = lax.dynamic_slice_in_dim(live_count, row_index, 1, 0)
            return (geometry(coord_block, spec_block, center_row, other_row, in_weight), center_row, other_row, live_row)

        def feature_row(row_index):
            (latent, harmonics, envelope), center_row, other_row, live_row = row_latent(row_index)
            return features(latent, harmonics, center_row, live_row, env_weight)
        stacked = lax.map(jax.checkpoint(feature_row), row_ids)
        features_all = jnp.moveaxis(stacked[:, :, 0], 0, 1)
        rounded = lax.optimization_barrier(features_all.astype(jnp.bfloat16)).astype(jnp.float32)
        through = features_all + lax.stop_gradient(rounded - features_all)
        feature_pad = wrap_pad(through, 1)

        def energy_row(row_index):
            (latent, harmonics, envelope), center_row, other_row, live_row = row_latent(row_index)
            feature_block = lax.dynamic_slice_in_dim(feature_pad, row_index, 3, 1)
            return energy(latent, envelope, feature_block, center_row, other_row, live_row, up_weight, out_weight)
        row_sums, row_atoms = lax.map(jax.checkpoint(energy_row), row_ids)
        return (jnp.sum(row_sums), row_atoms[:, 0])
    (energy_total, atom_energy), gradient = jax.value_and_grad(total, has_aux=True)(coords)
    return (atom_energy, -gradient)
```

```python
import jax
import jax.numpy as jnp
from jax import lax
from jax.experimental import pallas as pl
from jax.experimental.pallas import tpu as pltpu
from jax.sharding import PartitionSpec as P

NB = 8
SPEC = 8
LAT = 128
CH = 32
SOFTEN = 0.01
CUTOFF = 3.5
COLS = 8
F32 = jnp.float32
BF16 = jnp.bfloat16
PI = 3.141592653589793


def halves(value):
    high = value.astype(BF16)
    low = (value - high.astype(F32)).astype(BF16)
    return high, low


def dot(left, right):
    return lax.dot_general(left, right, (((1,), (0,)), ((), ())), preferred_element_type=F32)


def dot_t(left, right):
    return lax.dot_general(left, right, (((1,), (1,)), ((), ())), preferred_element_type=F32)


def t_dot(left, right):
    return lax.dot_general(left, right, (((0,), (0,)), ((), ())), preferred_element_type=F32)


def both(value):
    return value[:, :128] + value[:, 128:]


def iota(shape, dim):
    return lax.broadcasted_iota(jnp.int32, shape, dim)


def flag(condition):
    return jnp.where(condition, 1.0, 0.0).astype(F32)


def kernel(
    low_ref, mid_ref, high_ref, in_ref, env_ref, up_ref, out_ref,
    energy_ref, force_ref,
    grid_s, rows_s, geo_s, w_first, w_cast, w_env, w_env_t, w_up, w_down, w_rad, w_out,
    lat_s, slope_s, harm_s, msg_s, feat_s, dfeat_s, dlat_s, hout_s, back_s, vec_s,
    dfi_s, dfj_s, hot_c_s, hot_a_s, hot_at_s,
):
    col0 = lax.axis_index("xy") * 2
    first_row = (lax.axis_index("gz") % 2) * 2 + 1

    lane = iota((128, 128), 1)
    sub = iota((128, 128), 0)
    w_in = in_ref[...]
    wr_hi, wr_lo = halves(w_in[0:8])
    wi_hi, wi_lo = halves(w_in[8:16])
    wj_hi, wj_lo = halves(w_in[16:24])
    lane8 = iota((8, 128), 1)
    sub8 = iota((8, 128), 0)
    spread = flag((lane8 // CH) == (sub8 % 4))
    first = jnp.concatenate(
        [x.astype(F32) for x in (wr_hi, wr_hi, wr_lo, wi_hi, wi_lo, wj_hi, wj_lo)], axis=0
    )
    w_first[0:56, 0:128] = first.astype(BF16)
    w_first[0:64, 128:256] = jnp.concatenate([jnp.zeros((56, 128), F32), spread], axis=0).astype(BF16)
    w_first[48:64, 0:128] = jnp.concatenate([wj_lo.astype(F32), jnp.zeros((8, 128), F32)], axis=0).astype(BF16)
    zero8 = jnp.zeros((8, 128), F32)
    for block, table in enumerate(
        (
            flag(sub8 == 2),
            flag(sub8 == 3),
            flag(sub8 == 4),
            flag((sub8 == 5) | (sub8 == 6)),
        )
    ):
        w_cast[:, 128 * block : 128 * block + 128] = jnp.concatenate([zero8, table], axis=0).astype(BF16)
    env = env_ref[...]
    env_hi, env_lo = halves(env)
    tile = flag((iota((CH, 128), 1) % CH) == iota((CH, 128), 0)).astype(BF16)
    env4_hi = dot(env_hi, tile)
    env4_lo = dot(env_lo, tile)
    zero = jnp.zeros((128, 128), BF16)
    w_env[0:128, 0:128] = env4_hi.astype(BF16)
    w_env[0:128, 128:256] = env4_lo.astype(BF16)
    w_env[128:256, 0:128] = env4_hi.astype(BF16)
    w_env[128:256, 128:256] = zero
    env4_hi_t = jnp.transpose(env4_hi).astype(BF16)
    env4_lo_t = jnp.transpose(env4_lo).astype(BF16)
    w_env_t[0:128, 0:128] = env4_hi_t
    w_env_t[0:128, 128:256] = env4_lo_t
    w_env_t[128:256, 0:128] = env4_hi_t
    w_env_t[128:256, 128:256] = zero
    up = up_ref[...]
    up_l = up[0:128]
    up_p = jnp.concatenate([up[128:160]] * 4, axis=0)
    for base, block in ((0, up_l), (256, up_p)):
        hi, lo = halves(block)
        w_up[base : base + 128, 0:128] = hi
        w_up[base : base + 128, 128:256] = lo
        w_up[base + 128 : base + 256, 0:128] = hi
        w_up[base + 128 : base + 256, 128:256] = zero
        hi, lo = halves(jnp.transpose(block))
        w_down[0:128, base : base + 128] = hi
        w_down[128:256, base : base + 128] = hi
        w_down[0:128, base + 128 : base + 256] = lo
        w_down[128:256, base + 128 : base + 256] = zero
    z8 = jnp.zeros((8, 128), F32)
    wr_hi32 = wr_hi.astype(F32)
    wr_lo32 = wr_lo.astype(F32)
    ones4 = flag((lane8 // CH) == sub8)
    for block, parts in enumerate(
        ((wr_hi32, wr_lo32, z8, z8), (wr_hi32, z8, z8, z8), (z8, z8, ones4, z8), (z8, z8, ones4, z8))
    ):
        w_rad[:, 128 * block : 128 * block + 128] = jnp.concatenate(parts, axis=0).astype(BF16)
    out_row = out_ref[...]
    out_hi, out_lo = halves(out_row)
    out_hi32 = out_hi.astype(F32)
    out_lo32 = out_lo.astype(F32)
    z1 = jnp.zeros((1, 128), F32)
    pad14 = jnp.zeros((14, 128), F32)
    w_out[:, 0:128] = jnp.concatenate([out_hi32, out_lo32, pad14], axis=0).astype(BF16)
    w_out[:, 128:256] = jnp.concatenate([out_hi32, z1, pad14], axis=0).astype(BF16)

    for source, start in ((low_ref, 0), (mid_ref, 4), (high_ref, 8)):
        for peer in range(8):
            for row in range(2):
                for col in range(2):
                    place = ((start + peer // 4 * 2 + row) * COLS + peer % 4 * 2 + col) * 8
                    grid_s[place : place + 8, :] = source[peer, row, col]

    def quantity(row, which):
        return grid_s[pl.ds((first_row + row) * 64 + which, 8, stride=8), :]

    tables = [[quantity(row, which) for which in range(4)] for row in range(8)]
    for f in range(6):
        center = quantity(f + 1, 4)
        other = quantity(f + 1, 5)
        count = quantity(f + 1, 6)
        center_i = center.astype(jnp.int32)
        other_i = other.astype(jnp.int32)
        place = other_i // 128
        atom = other_i % 128
        at_i = [jnp.take_along_axis(tables[f + 1][which], center_i, axis=1) for which in range(4)]
        at_j = [jnp.zeros((8, 128), F32) for _ in range(4)]
        for offset in range(9):
            dr, dc = offset // 3 - 1, offset % 3 - 1
            here = place == offset
            for which in range(4):
                table = tables[f + 1 + dr][which]
                if dc:
                    table = pltpu.roll(table, (-dc) % 8, 0)
                value = jnp.take_along_axis(table, atom, axis=1)
                if which == 0:
                    value = value + float(dr)
                if which == 1:
                    value = value + float(dc)
                at_j[which] = jnp.where(here, value, at_j[which])
        dz, dx, dy = (at_j[which] - at_i[which] for which in range(3))
        distance = jnp.sqrt(dz * dz + dx * dx + dy * dy + SOFTEN)
        inverse = 1.0 / distance
        scaled = distance * (1.0 / CUTOFF)
        inner = 1.0 - scaled * scaled
        envelope = inner * inner
        slope = (-4.0 / CUTOFF) * inner * scaled
        live = flag(iota((8, 128), 1).astype(F32) < count)
        angle = PI * scaled
        sine, cosine = jnp.sin(angle), jnp.cos(angle)
        base = f * COLS * 32

        def put(which, value):
            rows_s[pl.ds(base + which, 8, stride=32), :] = value

        def split_put(which, gap, value):
            high = value.astype(BF16).astype(F32)
            put(which, high)
            put(which + gap, value - high)

        s_old, s_now = jnp.zeros_like(sine), sine
        c_old, c_now = jnp.ones_like(sine), cosine
        scale = inverse * envelope
        slope_scale = inverse * slope - inverse * scale
        for k in range(1, NB + 1):
            split_put(k - 1, 8, s_now * scale)
            geo_s[f, k - 1] = (k * PI / CUTOFF) * c_now * scale + s_now * slope_scale
            s_old, s_now = s_now, 2.0 * cosine * s_now - s_old
            c_old, c_now = c_now, 2.0 * cosine * c_now - c_old
        for m, value in enumerate((live, live * dz * inverse, live * dx * inverse, live * dy * inverse)):
            split_put(16 + m, 4, value)
        put(24, at_i[3])
        put(25, at_j[3])
        put(26, center)
        put(27, atom.astype(F32))
        put(28, place.astype(F32))
        split_put(29, 1, envelope * live)
        put(31, live)
        for which, value in enumerate((dz, dx, dy, inverse, live, slope, envelope)):
            geo_s[f, 8 + which] = value

    def slot(f, i):
        return f * COLS + ((col0 + (i + COLS - 2)) & (COLS - 1))

    def bin_rows(f, i, first, size):
        return rows_s[pl.ds(slot(f, i) * 32 + first, size), :]

    lanes = iota((128, 128), 1).astype(F32).astype(BF16)
    subs = iota((128, 128), 0).astype(F32).astype(BF16)
    one = jnp.ones((128, 128), BF16)

    def hot_rows(row):
        wide = jnp.broadcast_to(row, (128, 128)).astype(BF16)
        return jnp.where(wide == subs, one, zero)

    def feature_group(f, cols):
        inputs = []
        for i in cols:
            rows = bin_rows(f, i, 0, 32)
            spec_i = flag(rows[24:25] == iota((8, 128), 0).astype(F32))
            spec_j = flag(rows[25:26] == iota((8, 128), 0).astype(F32))
            inputs.append(jnp.concatenate(
                [rows[0:16], rows[0:8], spec_i, spec_i, spec_j, spec_j, rows[16:24]], axis=0
            ).astype(BF16))
        mixed = t_dot(jnp.concatenate(inputs, axis=1), w_first[...])
        pre, harm = mixed[:, :128], mixed[:, 128:]
        gate = 0.5 + 0.5 * jnp.tanh(0.5 * pre)
        latent = pre * gate
        lat = jnp.concatenate(halves(latent), axis=1)
        weights = both(dot(lat, w_env[...]))
        slope = gate + latent * (1.0 - gate)
        high, low = halves(weights * harm)
        for n, i in enumerate(cols):
            part = slice(128 * n, 128 * n + 128)
            message = jnp.concatenate([high[part], low[part]], axis=0)
            hot = hot_rows(bin_rows(f, i, 26, 1))
            feat = dot(jnp.concatenate([hot, hot], axis=1), message)
            lat_s[f, i] = lat[part]
            feat_s[f, i] = feat.astype(BF16)
            if 1 <= i <= 4:
                slope_s[f, i - 1] = slope[part]
                harm_s[f, i - 1] = harm[part]
                msg_s[f, i - 1] = weights[part]

    def feature_step(f, carry):
        for group in FEATURE_GROUPS:
            feature_group(f, group)
        return carry

    lax.fori_loop(0, 6, feature_step, 0)

    def cast(f, i):
        return t_dot(bin_rows(f, i, 16, 16).astype(BF16), w_cast[...])

    def energy_group(f, cols, reach, inside_row):
        feat_i, feat_j, weight, hots = [], [], [], []
        for i in cols:
            inside = inside_row and 1 <= i <= 4
            wide = cast(f, i)
            narrow = wide[:, :384].astype(BF16)
            center, atom, place = narrow[:, :128], narrow[:, 128:256], narrow[:, 256:]
            weight.append(wide[:, 384:])
            hot_c = jnp.where(center == lanes, one, zero)
            hot_a = jnp.where(atom == lanes, one, zero)
            feat_i.append(dot(hot_c, feat_s[f, i]))
            columns, tables_j = [], []
            for target, code in reach:
                for dc in (-1, 0, 1):
                    if inside or 1 <= i + dc <= 4:
                        columns.append(jnp.where(place == jnp.asarray(code + (dc + 1), F32).astype(BF16), hot_a, zero))
                        tables_j.append(feat_s[target, i + dc])
            feat_j.append(dot(jnp.concatenate(columns, axis=1), jnp.concatenate(tables_j, axis=0)))
            hots.append(hot_c)
            if inside:
                hot_c_s[f, i - 1] = hot_c
                hot_a_s[f, i - 1] = hot_a
            hot_at_s[f, i] = hot_rows(bin_rows(f, i, 27, 1))
        feat_i = jnp.concatenate(feat_i, axis=0)
        feat_j = jnp.concatenate(feat_j, axis=0)
        weight = jnp.concatenate(weight, axis=0)
        lat = jnp.concatenate([lat_s[f, i] for i in cols], axis=0)
        prod = jnp.concatenate(halves(feat_i * feat_j), axis=1)
        pre = both(dot(jnp.concatenate([lat, prod], axis=1), w_up[...]))
        gate = 0.5 + 0.5 * jnp.tanh(0.5 * pre)
        hidden = pre * gate
        d_pre = out_ref[...] * (gate + hidden * (1.0 - gate)) * weight
        d_pre = jnp.concatenate(halves(d_pre), axis=1)
        within = inside_row and 1 <= cols[0] <= 4
        if within:
            down = dot(d_pre, w_down[...])
            d_lat = both(down[:, :256])
            d_prod = both(down[:, 256:])
            hid = jnp.concatenate(halves(hidden), axis=1)
            readout = dot_t(w_out[...], hid)
            d_i = (d_prod * feat_j).astype(BF16)
        else:
            d_prod = both(dot(d_pre, w_down[:, 256:]))
        d_j = (d_prod * feat_i).astype(BF16)
        for n, i in enumerate(cols):
            part = slice(128 * n, 128 * n + 128)
            dfj_s[f, i] = d_j[part]
            if within:
                dfi_s[f, i - 1] = d_i[part]
                dlat_s[f, i - 1] = d_lat[part]
                value = readout[0:1, part] + readout[1:2, part]
                hout_s[pl.ds((f * 4 + (i - 1)) * 8, 8), :] = jnp.broadcast_to(value, (8, 128))
                if i in (2, 3):
                    rows = bin_rows(f, i, 24, 8)
                    edge = value * (rows[5:6] + rows[6:7])
                    high = edge.astype(BF16).astype(F32)
                    parts = jnp.concatenate([high, edge - high, jnp.zeros((14, 128), F32)], axis=0)
                    summed = dot(parts.astype(BF16), hots[n])
                    energy_ref[jnp.clip(f - 2, 0, 1), pl.ds(i - 2, 1), :] = jnp.where(
                        (f == 2) | (f == 3), summed[0:1] + summed[1:2],
                        energy_ref[jnp.clip(f - 2, 0, 1), pl.ds(i - 2, 1), :])

    def energy_step(f, carry):
        reach = [(f + dr, 3.0 * (dr + 1)) for dr in (-1, 0, 1)]
        for group in ENERGY_GROUPS:
            energy_group(f, group, reach, True)
        return carry

    def rim_step(t, carry):
        for group in RIM_GROUPS:
            energy_group(5 * t, group, [(1 + 3 * t, 6.0 - 6.0 * t.astype(F32))], False)
        return carry

    energy_ref[...] = jnp.zeros_like(energy_ref)
    lax.fori_loop(1, 5, energy_step, 0)
    lax.fori_loop(0, 2, rim_step, 0)

    def backward_group(f, cols):
        d_msg = []
        for i in cols:
            columns, terms = [hot_rows(bin_rows(f, i, 26, 1))], [dfi_s[f, i - 1]]
            for dr in (-1, 0, 1):
                for dc in (-1, 0, 1):
                    code = float(3 * (1 - dr) + (1 - dc))
                    mask = flag(bin_rows(f + dr, i + dc, 28, 1) == code)
                    mask = jnp.broadcast_to(mask, (128, 128)).astype(BF16)
                    columns.append(hot_at_s[f + dr, i + dc] * mask)
                    terms.append(dfj_s[f + dr, i + dc])
            d_feat = dot(jnp.concatenate(columns, axis=1), jnp.concatenate(terms, axis=0))
            hot = hot_c_s[f, i - 1]
            d_msg.append(dot(jnp.concatenate([hot, hot], axis=1), jnp.concatenate(halves(d_feat), axis=0)))
        d_msg = jnp.concatenate(d_msg, axis=0)
        gather = lambda ref: jnp.concatenate([ref[f, i - 1] for i in cols], axis=0)
        d_weight = jnp.concatenate(halves(d_msg * gather(harm_s)), axis=1)
        d_lat = both(dot(d_weight, w_env_t[...])) + gather(dlat_s)
        d_pre = jnp.concatenate(
            halves(d_lat * gather(slope_s)) + halves(d_msg * gather(msg_s)), axis=1
        )
        rows = dot_t(w_rad[...], d_pre)
        result = jnp.concatenate([rows[0:8] + rows[8:16], rows[16:24]], axis=0)
        for n, i in enumerate(cols):
            back_s[pl.ds(slot(f, i) * 16, 16), :] = result[:, 128 * n : 128 * n + 128]

    def backward_step(f, carry):
        for group in BACK_GROUPS:
            backward_group(f, group)
        return carry

    back_s[...] = jnp.zeros_like(back_s)
    lax.fori_loop(1, 5, backward_step, 0)

    for f in range(1, 5):
        def got(which):
            return back_s[pl.ds(f * COLS * 16 + which, 8, stride=16), :]

        dz, dx, dy, inverse, live, slope = (geo_s[f, 8 + which] for which in range(6))
        d_dist = jnp.zeros((8, 128), F32)
        for k in range(NB):
            d_dist = d_dist + got(k) * geo_s[f, k]
        readout = jnp.zeros((8, 128), F32)
        col = iota((8, 128), 0)
        for i in range(1, 5):
            value = hout_s[(f * 4 + i - 1) * 8 : (f * 4 + i - 1) * 8 + 8, :]
            readout = jnp.where(col == ((col0 + (i + COLS - 2)) & (COLS - 1)), value, readout)
        d_dist = d_dist + readout * live * slope
        hz, hx, hy = (got(8 + m) * live for m in (1, 2, 3))
        d_dist = d_dist - (hz * dz + hx * dx + hy * dy) * inverse * inverse
        along = d_dist * inverse
        for axis, (delta, own) in enumerate(((dz, hz), (dx, hx), (dy, hy))):
            value = along * delta + own * inverse
            high = value.astype(BF16).astype(F32)
            vec_s[pl.ds(f * COLS * 8 + 2 * axis, 8, stride=8), :] = high
            vec_s[pl.ds(f * COLS * 8 + 2 * axis + 1, 8, stride=8), :] = value - high
        for spare in (6, 7):
            vec_s[pl.ds(f * COLS * 8 + spare, 8, stride=8), :] = jnp.zeros((8, 128), F32)

    total = [[jnp.zeros((8, 128), F32) for _ in range(2)] for _ in range(2)]
    for f in range(1, 5):
        for i in range(1, 5):
            vec = vec_s[pl.ds(slot(f, i) * 8, 8), :]
            place = bin_rows(f, i, 28, 1)
            targets = [(dr, dc) for dr in (-1, 0, 1) for dc in (-1, 0, 1) if 2 <= i + dc <= 3 and 2 <= f + dr <= 3]
            parts = [vec * flag(place == float((dr + 1) * 3 + dc + 1)) for dr, dc in targets]
            if len(parts) % 2:
                parts.append(jnp.zeros((8, 128), F32))
            moved = dot(jnp.concatenate(parts, axis=0).astype(BF16), hot_a_s[f, i - 1])
            for index, (dr, dc) in enumerate(targets):
                total[f + dr - 2][i + dc - 2] -= moved[8 * index : 8 * index + 8]
            if i in (2, 3) and f in (2, 3):
                centered = jnp.concatenate([vec, jnp.zeros((8, 128), F32)], axis=0).astype(BF16)
                total[f - 2][i - 2] += dot(centered, hot_c_s[f, i - 1])[0:8]
    for row in range(2):
        for col in range(2):
            value = total[row][col]
            for axis in range(3):
                force_ref[axis, row, pl.ds(col, 1), :] = (
                    value[2 * axis : 2 * axis + 1] + value[2 * axis + 1 : 2 * axis + 2]
                )


FEATURE_GROUPS = ((0, 1, 2, 3, 4, 5),)
ENERGY_GROUPS = ((1, 2, 3, 4), (0, 5))
RIM_GROUPS = ((0, 1, 2, 3, 4, 5),)
BACK_GROUPS = ((1, 2, 3, 4),)


def compute(low, mid, high, in_weight, env_weight, up_weight, out_weight):
    return pl.pallas_call(
        kernel,
        out_shape=(
            jax.ShapeDtypeStruct((2, 2, 128), F32),
            jax.ShapeDtypeStruct((3, 2, 2, 128), F32),
        ),
        in_specs=[pl.BlockSpec(memory_space=pltpu.VMEM)] * 7,
        out_specs=[pl.BlockSpec(memory_space=pltpu.VMEM)] * 2,
        scratch_shapes=[
            pltpu.VMEM((12 * COLS * 8, 128), F32),
            pltpu.VMEM((6 * COLS * 32, 128), F32),
            pltpu.VMEM((6, 16, COLS, 128), F32),
            pltpu.VMEM((64, 256), BF16),
            pltpu.VMEM((16, 512), BF16),
            pltpu.VMEM((256, 256), BF16),
            pltpu.VMEM((256, 256), BF16),
            pltpu.VMEM((512, 256), BF16),
            pltpu.VMEM((256, 512), BF16),
            pltpu.VMEM((32, 512), BF16),
            pltpu.VMEM((16, 256), BF16),
            pltpu.VMEM((6, 6, 128, 256), BF16),
            pltpu.VMEM((6, 4, 128, 128), F32),
            pltpu.VMEM((6, 4, 128, 128), F32),
            pltpu.VMEM((6, 4, 128, 128), F32),
            pltpu.VMEM((6, 6, 128, 128), BF16),
            pltpu.VMEM((8, 128), F32),
            pltpu.VMEM((6, 4, 128, 128), F32),
            pltpu.VMEM((6 * 4 * 8, 128), F32),
            pltpu.VMEM((6 * COLS * 16, 128), F32),
            pltpu.VMEM((6 * COLS * 8, 128), F32),
            pltpu.VMEM((6, 4, 128, 128), BF16),
            pltpu.VMEM((6, 6, 128, 128), BF16),
            pltpu.VMEM((6, 4, 128, 128), BF16),
            pltpu.VMEM((6, 4, 128, 128), BF16),
            pltpu.VMEM((6, 6, 128, 128), BF16),
        ],
        compiler_params=pltpu.CompilerParams(vmem_limit_bytes=40 * 1024 * 1024),
        name="potential",
    )(low, mid, high, in_weight, env_weight, up_weight, out_weight)


def pack_kernel(coords_ref, species_ref, centers_ref, others_ref, live_ref, packed_ref):
    for row in range(2):
        for col in range(2):
            at = pl.ds(col, 1)
            tile = jnp.concatenate(
                [coords_ref[axis, row, at, :] for axis in range(3)]
                + [ref[row, at, :].astype(F32) for ref in (species_ref, centers_ref, others_ref)]
                + [jnp.full((1, 128), live_ref[row, col], jnp.int32).astype(F32), jnp.zeros((1, 128), F32)],
                axis=0,
            )
            for peer in range(8):
                packed_ref[peer, row, col] = tile


def pack(coords, species, centers, others, live_count):
    return pl.pallas_call(
        pack_kernel,
        out_shape=jax.ShapeDtypeStruct((8, 2, 2, 8, 128), F32),
        in_specs=[pl.BlockSpec(memory_space=pltpu.VMEM)] * 4 + [pl.BlockSpec(memory_space=pltpu.SMEM)],
        out_specs=pl.BlockSpec(memory_space=pltpu.VMEM),
        name="pack",
    )(coords, species, centers, others, live_count)


def shift(value, axis, step):
    count = lax.axis_size(axis)
    return lax.ppermute(value, axis, [(i, (i + step) % count) for i in range(count)])


def body(
    coords, species, centers, others, live_count, in_weight, env_weight, up_weight, out_weight
):
    packed = pack(coords, species, centers, others, live_count)
    depth, width = lax.axis_size("gz"), lax.axis_size("xy")
    chips = [
        [(2 * chip + core) * width + place for core in range(2) for place in range(width)]
        for chip in range(depth // 2)
    ]
    mid = lax.all_to_all(packed, ("gz", "xy"), 0, 0, tiled=True, axis_index_groups=chips)
    low = shift(mid, "gz", 2)
    high = shift(mid, "gz", -2)
    return compute(low, mid, high, in_weight, env_weight, up_weight, out_weight.reshape(1, -1))


def solution(mesh):
    in_specs = (
        P(None, "gz", "xy", None),
        P("gz", "xy", None),
        P("gz", "xy", None),
        P("gz", "xy", None),
        P("gz", "xy"),
        P(),
        P(),
        P(),
        P(),
    )
    out_specs = (P("gz", "xy", None), P(None, "gz", "xy", None))
    return jax.shard_map(body, mesh=mesh, in_specs=in_specs, out_specs=out_specs, check_vma=False)
```

```python
import jax
import jax.numpy as jnp
from jax import lax
from jax.experimental import pallas as pl
from jax.experimental.pallas import tpu as pltpu
from jax.sharding import PartitionSpec as P

NB = 8
SPEC = 8
LAT = 128
CH = 32
SOFTEN = 0.01
CUTOFF = 3.5
COLS = 8
F32 = jnp.float32
BF16 = jnp.bfloat16
PI = 3.141592653589793


def halves(value):
    high = value.astype(BF16)
    low = (value - high.astype(F32)).astype(BF16)
    return high, low


def dot(left, right):
    return lax.dot_general(left, right, (((1,), (0,)), ((), ())), preferred_element_type=F32)


def dot_t(left, right):
    return lax.dot_general(left, right, (((1,), (1,)), ((), ())), preferred_element_type=F32)


def t_dot(left, right):
    return lax.dot_general(left, right, (((0,), (0,)), ((), ())), preferred_element_type=F32)


def both(value):
    return value[:, :128] + value[:, 128:]


def iota(shape, dim):
    return lax.broadcasted_iota(jnp.int32, shape, dim)


def flag(condition):
    return jnp.where(condition, 1.0, 0.0).astype(F32)


def kernel(
    low_ref, mid_ref, high_ref, in_ref, env_ref, up_ref, out_ref,
    energy_ref, force_ref,
    grid_s, rows_s, geo_s, w_first, w_env, w_env_t, w_up, w_down, w_rad, w_out,
    lat_s, slope_s, harm_s, msg_s, feat_s, dfeat_s, dlat_s, hout_s, back_s, vec_s,
    dfi_s, dfj_s, hot_c_s, hot_a_s, hot_at_s, index_s, weight_s,
):
    col0 = lax.axis_index("xy") * 2
    first_row = (lax.axis_index("gz") % 2) * 2 + 1

    lane = iota((128, 128), 1)
    sub = iota((128, 128), 0)
    w_in = in_ref[...]
    wr_hi, wr_lo = halves(w_in[0:8])
    wi_hi, wi_lo = halves(w_in[8:16])
    wj_hi, wj_lo = halves(w_in[16:24])
    lane8 = iota((8, 128), 1)
    sub8 = iota((8, 128), 0)
    spread = flag((lane8 // CH) == (sub8 % 4))
    first = jnp.concatenate(
        [x.astype(F32) for x in (wr_hi, wr_hi, wr_lo, wi_hi, wi_lo, wj_hi, wj_lo)], axis=0
    )
    w_first[:, 0:128] = jnp.concatenate([first, jnp.zeros((24, 128), F32)], axis=0).astype(BF16)
    w_first[:, 128:256] = jnp.concatenate(
        [jnp.zeros((56, 128), F32), spread, jnp.zeros((16, 128), F32)], axis=0
    ).astype(BF16)
    for block, table in enumerate(
        (
            flag(sub8 == 2),
            flag(sub8 == 3),
            flag(sub8 == 4),
            flag((sub8 == 5) | (sub8 == 6)),
        )
    ):
        w_first[:, 128 * block + 256 : 128 * block + 384] = jnp.concatenate(
            [jnp.zeros((64, 128), F32), table, jnp.zeros((8, 128), F32)], axis=0
        ).astype(BF16)
    env = env_ref[...]
    env_hi, env_lo = halves(env)
    tile = flag((iota((CH, 128), 1) % CH) == iota((CH, 128), 0)).astype(BF16)
    env4_hi = dot(env_hi, tile)
    env4_lo = dot(env_lo, tile)
    zero = jnp.zeros((128, 128), BF16)
    w_env[0:128, 0:128] = env4_hi.astype(BF16)
    w_env[0:128, 128:256] = env4_lo.astype(BF16)
    w_env[128:256, 0:128] = env4_hi.astype(BF16)
    w_env[128:256, 128:256] = zero
    env4_hi_t = jnp.transpose(env4_hi).astype(BF16)
    env4_lo_t = jnp.transpose(env4_lo).astype(BF16)
    w_env_t[0:128, 0:128] = env4_hi_t
    w_env_t[0:128, 128:256] = env4_lo_t
    w_env_t[128:256, 0:128] = env4_hi_t
    w_env_t[128:256, 128:256] = zero
    up = up_ref[...]
    up_l = up[0:128]
    up_p = jnp.concatenate([up[128:160]] * 4, axis=0)
    for base, block in ((0, up_l), (256, up_p)):
        hi, lo = halves(block)
        w_up[base : base + 128, 0:128] = hi
        w_up[base : base + 128, 128:256] = lo
        w_up[base + 128 : base + 256, 0:128] = hi
        w_up[base + 128 : base + 256, 128:256] = zero
        hi, lo = halves(jnp.transpose(block))
        w_down[0:128, base : base + 128] = hi
        w_down[128:256, base : base + 128] = hi
        w_down[0:128, base + 128 : base + 256] = lo
        w_down[128:256, base + 128 : base + 256] = zero
    z8 = jnp.zeros((8, 128), F32)
    wr_hi32 = wr_hi.astype(F32)
    wr_lo32 = wr_lo.astype(F32)
    ones4 = flag((lane8 // CH) == sub8)
    for block, parts in enumerate(
        ((wr_hi32, wr_lo32, z8, z8), (wr_hi32, z8, z8, z8), (z8, z8, ones4, z8), (z8, z8, ones4, z8))
    ):
        w_rad[:, 128 * block : 128 * block + 128] = jnp.concatenate(parts, axis=0).astype(BF16)
    out_row = out_ref[...]
    out_hi, out_lo = halves(out_row)
    out_hi32 = out_hi.astype(F32)
    out_lo32 = out_lo.astype(F32)
    z1 = jnp.zeros((1, 128), F32)
    pad14 = jnp.zeros((14, 128), F32)
    w_out[:, 0:128] = jnp.concatenate([out_hi32, out_lo32, pad14], axis=0).astype(BF16)
    w_out[:, 128:256] = jnp.concatenate([out_hi32, z1, pad14], axis=0).astype(BF16)

    for source, start in ((low_ref, 0), (mid_ref, 4), (high_ref, 8)):
        for peer in range(8):
            for row in range(2):
                for col in range(2):
                    place = ((start + peer // 4 * 2 + row) * COLS + peer % 4 * 2 + col) * 8
                    size = source.shape[3]
                    grid_s[place : place + size, :] = source[peer, row, col]

    def quantity(row, which):
        return grid_s[pl.ds((first_row + row) * 64 + which, 8, stride=8), :]

    tables = [[quantity(row, which) for which in range(4)] for row in range(8)]
    for f in range(6):
        center = quantity(f + 1, 4)
        other = quantity(f + 1, 5)
        count = quantity(f + 1, 6)
        center_i = center.astype(jnp.int32)
        other_i = other.astype(jnp.int32)
        place = other_i // 128
        atom = other_i % 128
        at_i = [jnp.take_along_axis(tables[f + 1][which], center_i, axis=1) for which in range(4)]
        at_j = [jnp.zeros((8, 128), F32) for _ in range(4)]
        for offset in range(9):
            dr, dc = offset // 3 - 1, offset % 3 - 1
            here = place == offset
            for which in range(4):
                table = tables[f + 1 + dr][which]
                if dc:
                    table = pltpu.roll(table, (-dc) % 8, 0)
                value = jnp.take_along_axis(table, atom, axis=1)
                if which == 0:
                    value = value + float(dr)
                if which == 1:
                    value = value + float(dc)
                at_j[which] = jnp.where(here, value, at_j[which])
        dz, dx, dy = (at_j[which] - at_i[which] for which in range(3))
        distance = jnp.sqrt(dz * dz + dx * dx + dy * dy + SOFTEN)
        inverse = 1.0 / distance
        scaled = distance * (1.0 / CUTOFF)
        inner = 1.0 - scaled * scaled
        envelope = inner * inner
        slope = (-4.0 / CUTOFF) * inner * scaled
        live = flag(iota((8, 128), 1).astype(F32) < count)
        angle = PI * scaled
        sine, cosine = jnp.sin(angle), jnp.cos(angle)
        base = f * COLS * 32

        def put(which, value):
            rows_s[pl.ds(base + which, 8, stride=32), :] = value

        def split_put(which, gap, value):
            high = value.astype(BF16).astype(F32)
            put(which, high)
            put(which + gap, value - high)

        s_old, s_now = jnp.zeros_like(sine), sine
        c_old, c_now = jnp.ones_like(sine), cosine
        scale = inverse * envelope
        slope_scale = inverse * slope - inverse * scale
        for k in range(1, NB + 1):
            split_put(k - 1, 8, s_now * scale)
            geo_s[f, k - 1] = (k * PI / CUTOFF) * c_now * scale + s_now * slope_scale
            s_old, s_now = s_now, 2.0 * cosine * s_now - s_old
            c_old, c_now = c_now, 2.0 * cosine * c_now - c_old
        for m, value in enumerate((live, live * dz * inverse, live * dx * inverse, live * dy * inverse)):
            split_put(16 + m, 4, value)
        put(24, at_i[3])
        put(25, at_j[3])
        put(26, center)
        put(27, atom.astype(F32))
        put(28, place.astype(F32))
        split_put(29, 1, envelope * live)
        put(31, live)
        for which, value in enumerate((dz, dx, dy, inverse, live, slope, envelope)):
            geo_s[f, 8 + which] = value

    def slot(f, i):
        return f * COLS + ((col0 + (i + COLS - 2)) & (COLS - 1))

    def bin_rows(f, i, first, size):
        return rows_s[pl.ds(slot(f, i) * 32 + first, size), :]

    lanes = iota((128, 128), 1).astype(F32).astype(BF16)
    subs = iota((128, 128), 0).astype(F32).astype(BF16)
    one = jnp.ones((128, 128), BF16)

    def hot_rows(row):
        wide = jnp.broadcast_to(row, (128, 128)).astype(BF16)
        return jnp.where(wide == subs, one, zero)

    def feature_group(f, cols):
        inputs = []
        for i in cols:
            rows = bin_rows(f, i, 0, 32)
            spec_i = flag(rows[24:25] == iota((8, 128), 0).astype(F32))
            spec_j = flag(rows[25:26] == iota((8, 128), 0).astype(F32))
            inputs.append(jnp.concatenate(
                [rows[0:16], rows[0:8], spec_i, spec_i, spec_j, spec_j, rows[16:32], jnp.zeros((8, 128), F32)],
                axis=0,
            ).astype(BF16))
        mixed = t_dot(jnp.concatenate(inputs, axis=1), w_first[...])
        pre, harm = mixed[:, :128], mixed[:, 128:256]
        narrow = mixed[:, 256:640].astype(BF16)
        gate = 0.5 + 0.5 * jnp.tanh(0.5 * pre)
        latent = pre * gate
        lat = jnp.concatenate(halves(latent), axis=1)
        weights = both(dot(lat, w_env[...]))
        slope = gate + latent * (1.0 - gate)
        high, low = halves(weights * harm)
        for n, i in enumerate(cols):
            part = slice(128 * n, 128 * n + 128)
            message = jnp.concatenate([high[part], low[part]], axis=0)
            hot = hot_rows(bin_rows(f, i, 26, 1))
            feat = dot(jnp.concatenate([hot, hot], axis=1), message)
            lat_s[f, i] = lat[part]
            index_s[f, i] = narrow[part]
            weight_s[f, i] = mixed[part, 640:]
            feat_s[f, i] = feat.astype(BF16)
            if 1 <= i <= 4:
                slope_s[f, i - 1] = slope[part]
                harm_s[f, i - 1] = harm[part]
                msg_s[f, i - 1] = weights[part]

    def feature_step(f, carry):
        for group in FEATURE_GROUPS:
            feature_group(f, group)
        return carry

    lax.fori_loop(0, 6, feature_step, 0)

    def energy_group(f, cols, reach, inside_row):
        feat_i, feat_j, weight, hots = [], [], [], []
        for i in cols:
            inside = inside_row and 1 <= i <= 4
            narrow = index_s[f, i]
            center, atom, place = narrow[:, :128], narrow[:, 128:256], narrow[:, 256:]
            weight.append(weight_s[f, i])
            hot_c = jnp.where(center == lanes, one, zero)
            hot_a = jnp.where(atom == lanes, one, zero)
            feat_i.append(dot(hot_c, feat_s[f, i]))
            columns, tables_j = [], []
            for target, code in reach:
                for dc in (-1, 0, 1):
                    if inside or 1 <= i + dc <= 4:
                        columns.append(jnp.where(place == jnp.asarray(code + (dc + 1), F32).astype(BF16), hot_a, zero))
                        tables_j.append(feat_s[target, i + dc])
            feat_j.append(dot(jnp.concatenate(columns, axis=1), jnp.concatenate(tables_j, axis=0)))
            hots.append(hot_c)
            if inside:
                hot_c_s[f, i - 1] = hot_c
                hot_a_s[f, i - 1] = hot_a
            hot_at_s[f, i] = hot_rows(bin_rows(f, i, 27, 1))
        feat_i = jnp.concatenate(feat_i, axis=0)
        feat_j = jnp.concatenate(feat_j, axis=0)
        weight = jnp.concatenate(weight, axis=0)
        lat = jnp.concatenate([lat_s[f, i] for i in cols], axis=0)
        prod = jnp.concatenate(halves(feat_i * feat_j), axis=1)
        pre = both(dot(jnp.concatenate([lat, prod], axis=1), w_up[...]))
        gate = 0.5 + 0.5 * jnp.tanh(0.5 * pre)
        hidden = pre * gate
        d_pre = out_ref[...] * (gate + hidden * (1.0 - gate)) * weight
        d_pre = jnp.concatenate(halves(d_pre), axis=1)
        within = inside_row and 1 <= cols[0] <= 4
        if within:
            down = dot(d_pre, w_down[...])
            d_lat = both(down[:, :256])
            d_prod = both(down[:, 256:])
            hid = jnp.concatenate(halves(hidden), axis=1)
            readout = dot_t(w_out[...], hid)
            d_i = jnp.concatenate(halves(d_prod * feat_j), axis=1)
        else:
            d_prod = both(dot(d_pre, w_down[:, 256:]))
        d_j = jnp.concatenate(halves(d_prod * feat_i), axis=1)
        for n, i in enumerate(cols):
            part = slice(128 * n, 128 * n + 128)
            dfj_s[f, i] = d_j[part]
            if within:
                dfi_s[f, i - 1] = d_i[part]
                dlat_s[f, i - 1] = d_lat[part]
                value = readout[0:1, part] + readout[1:2, part]
                hout_s[pl.ds((f * 4 + (i - 1)) * 8, 8), :] = jnp.broadcast_to(value, (8, 128))
                if i in (2, 3):
                    rows = bin_rows(f, i, 24, 8)
                    edge = value * (rows[5:6] + rows[6:7])
                    high = edge.astype(BF16).astype(F32)
                    parts = jnp.concatenate([high, edge - high, jnp.zeros((14, 128), F32)], axis=0)
                    summed = dot(parts.astype(BF16), hots[n])
                    energy_ref[jnp.clip(f - 2, 0, 1), pl.ds(i - 2, 1), :] = jnp.where(
                        (f == 2) | (f == 3), summed[0:1] + summed[1:2],
                        energy_ref[jnp.clip(f - 2, 0, 1), pl.ds(i - 2, 1), :])

    def energy_step(f, carry):
        reach = [(f + dr, 3.0 * (dr + 1)) for dr in (-1, 0, 1)]
        for group in ENERGY_GROUPS:
            energy_group(f, group, reach, True)
        return carry

    def rim_step(t, carry):
        for group in RIM_GROUPS:
            energy_group(5 * t, group, [(1 + 3 * t, 6.0 - 6.0 * t.astype(F32))], False)
        return carry

    energy_ref[...] = jnp.zeros_like(energy_ref)
    lax.fori_loop(1, 5, energy_step, 0)
    lax.fori_loop(0, 2, rim_step, 0)

    def backward_group(f, cols):
        d_msg = []
        for i in cols:
            columns, terms = [hot_rows(bin_rows(f, i, 26, 1))], [dfi_s[f, i - 1]]
            for dr in (-1, 0, 1):
                for dc in (-1, 0, 1):
                    code = float(3 * (1 - dr) + (1 - dc))
                    mask = flag(bin_rows(f + dr, i + dc, 28, 1) == code)
                    mask = jnp.broadcast_to(mask, (128, 128)).astype(BF16)
                    columns.append(hot_at_s[f + dr, i + dc] * mask)
                    terms.append(dfj_s[f + dr, i + dc])
            d_feat = both(dot(jnp.concatenate(columns, axis=1), jnp.concatenate(terms, axis=0)))
            hot = hot_c_s[f, i - 1]
            d_msg.append(dot(jnp.concatenate([hot, hot], axis=1), jnp.concatenate(halves(d_feat), axis=0)))
        d_msg = jnp.concatenate(d_msg, axis=0)
        gather = lambda ref: jnp.concatenate([ref[f, i - 1] for i in cols], axis=0)
        d_weight = jnp.concatenate(halves(d_msg * gather(harm_s)), axis=1)
        d_lat = both(dot(d_weight, w_env_t[...])) + gather(dlat_s)
        d_pre = jnp.concatenate(
            halves(d_lat * gather(slope_s)) + halves(d_msg * gather(msg_s)), axis=1
        )
        rows = dot_t(w_rad[...], d_pre)
        result = jnp.concatenate([rows[0:8] + rows[8:16], rows[16:24]], axis=0)
        for n, i in enumerate(cols):
            back_s[pl.ds(slot(f, i) * 16, 16), :] = result[:, 128 * n : 128 * n + 128]

    def backward_step(f, carry):
        for group in BACK_GROUPS:
            backward_group(f, group)
        return carry

    back_s[...] = jnp.zeros_like(back_s)
    lax.fori_loop(1, 5, backward_step, 0)

    for f in range(1, 5):
        def got(which):
            return back_s[pl.ds(f * COLS * 16 + which, 8, stride=16), :]

        dz, dx, dy, inverse, live, slope = (geo_s[f, 8 + which] for which in range(6))
        d_dist = jnp.zeros((8, 128), F32)
        for k in range(NB):
            d_dist = d_dist + got(k) * geo_s[f, k]
        readout = jnp.zeros((8, 128), F32)
        col = iota((8, 128), 0)
        for i in range(1, 5):
            value = hout_s[(f * 4 + i - 1) * 8 : (f * 4 + i - 1) * 8 + 8, :]
            readout = jnp.where(col == ((col0 + (i + COLS - 2)) & (COLS - 1)), value, readout)
        d_dist = d_dist + readout * live * slope
        hz, hx, hy = (got(8 + m) * live for m in (1, 2, 3))
        d_dist = d_dist - (hz * dz + hx * dx + hy * dy) * inverse * inverse
        along = d_dist * inverse
        for axis, (delta, own) in enumerate(((dz, hz), (dx, hx), (dy, hy))):
            value = along * delta + own * inverse
            high = value.astype(BF16).astype(F32)
            vec_s[pl.ds(f * COLS * 8 + 2 * axis, 8, stride=8), :] = high
            vec_s[pl.ds(f * COLS * 8 + 2 * axis + 1, 8, stride=8), :] = value - high
        for spare in (6, 7):
            vec_s[pl.ds(f * COLS * 8 + spare, 8, stride=8), :] = jnp.zeros((8, 128), F32)

    total = [[jnp.zeros((8, 128), F32) for _ in range(2)] for _ in range(2)]
    for f in range(1, 5):
        for i in range(1, 5):
            vec = vec_s[pl.ds(slot(f, i) * 8, 8), :]
            place = bin_rows(f, i, 28, 1)
            targets = [(dr, dc) for dr in (-1, 0, 1) for dc in (-1, 0, 1) if 2 <= i + dc <= 3 and 2 <= f + dr <= 3]
            parts = [vec * flag(place == float((dr + 1) * 3 + dc + 1)) for dr, dc in targets]
            if len(parts) % 2:
                parts.append(jnp.zeros((8, 128), F32))
            moved = dot(jnp.concatenate(parts, axis=0).astype(BF16), hot_a_s[f, i - 1])
            for index, (dr, dc) in enumerate(targets):
                total[f + dr - 2][i + dc - 2] -= moved[8 * index : 8 * index + 8]
            if i in (2, 3) and f in (2, 3):
                centered = jnp.concatenate([vec, jnp.zeros((8, 128), F32)], axis=0).astype(BF16)
                total[f - 2][i - 2] += dot(centered, hot_c_s[f, i - 1])[0:8]
    for row in range(2):
        for col in range(2):
            value = total[row][col]
            for axis in range(3):
                force_ref[axis, row, pl.ds(col, 1), :] = (
                    value[2 * axis : 2 * axis + 1] + value[2 * axis + 1 : 2 * axis + 2]
                )


FEATURE_GROUPS = ((0, 1, 2, 3, 4, 5),)
ENERGY_GROUPS = ((1, 2, 3, 4), (0, 5))
RIM_GROUPS = ((0, 1, 2, 3, 4, 5),)
BACK_GROUPS = ((1, 2, 3, 4),)


def compute(low, mid, high, in_weight, env_weight, up_weight, out_weight):
    return pl.pallas_call(
        kernel,
        out_shape=(
            jax.ShapeDtypeStruct((2, 2, 128), F32),
            jax.ShapeDtypeStruct((3, 2, 2, 128), F32),
        ),
        in_specs=[pl.BlockSpec(memory_space=pltpu.VMEM)] * 7,
        out_specs=[pl.BlockSpec(memory_space=pltpu.VMEM)] * 2,
        scratch_shapes=[
            pltpu.VMEM((12 * COLS * 8, 128), F32),
            pltpu.VMEM((6 * COLS * 32, 128), F32),
            pltpu.VMEM((6, 16, COLS, 128), F32),
            pltpu.VMEM((80, 768), BF16),
            pltpu.VMEM((256, 256), BF16),
            pltpu.VMEM((256, 256), BF16),
            pltpu.VMEM((512, 256), BF16),
            pltpu.VMEM((256, 512), BF16),
            pltpu.VMEM((32, 512), BF16),
            pltpu.VMEM((16, 256), BF16),
            pltpu.VMEM((6, 6, 128, 256), BF16),
            pltpu.VMEM((6, 4, 128, 128), F32),
            pltpu.VMEM((6, 4, 128, 128), F32),
            pltpu.VMEM((6, 4, 128, 128), F32),
            pltpu.VMEM((6, 6, 128, 128), BF16),
            pltpu.VMEM((8, 128), F32),
            pltpu.VMEM((6, 4, 128, 128), F32),
            pltpu.VMEM((6 * 4 * 8, 128), F32),
            pltpu.VMEM((6 * COLS * 16, 128), F32),
            pltpu.VMEM((6 * COLS * 8, 128), F32),
            pltpu.VMEM((6, 4, 128, 256), BF16),
            pltpu.VMEM((6, 6, 128, 256), BF16),
            pltpu.VMEM((6, 4, 128, 128), BF16),
            pltpu.VMEM((6, 4, 128, 128), BF16),
            pltpu.VMEM((6, 6, 128, 128), BF16),
            pltpu.VMEM((6, 6, 128, 384), BF16),
            pltpu.VMEM((6, 6, 128, 128), F32),
        ],
        compiler_params=pltpu.CompilerParams(vmem_limit_bytes=40 * 1024 * 1024),
        name="potential",
    )(low, mid, high, in_weight, env_weight, up_weight, out_weight)


def pack_kernel(coords_ref, species_ref, centers_ref, others_ref, live_ref, packed_ref):
    for row in range(2):
        for col in range(2):
            at = pl.ds(col, 1)
            tile = jnp.concatenate(
                [coords_ref[axis, row, at, :] for axis in range(3)]
                + [ref[row, at, :].astype(F32) for ref in (species_ref, centers_ref, others_ref)]
                + [jnp.full((1, 128), live_ref[row, col], jnp.int32).astype(F32), jnp.zeros((1, 128), F32)],
                axis=0,
            )
            for peer in range(8):
                packed_ref[peer, row, col] = tile


def pack(coords, species, centers, others, live_count):
    return pl.pallas_call(
        pack_kernel,
        out_shape=jax.ShapeDtypeStruct((8, 2, 2, 8, 128), F32),
        in_specs=[pl.BlockSpec(memory_space=pltpu.VMEM)] * 4 + [pl.BlockSpec(memory_space=pltpu.SMEM)],
        out_specs=pl.BlockSpec(memory_space=pltpu.VMEM),
        name="pack",
    )(coords, species, centers, others, live_count)


def shift(value, axis, step):
    count = lax.axis_size(axis)
    return lax.ppermute(value, axis, [(i, (i + step) % count) for i in range(count)])


def body(
    coords, species, centers, others, live_count, in_weight, env_weight, up_weight, out_weight
):
    packed = pack(coords, species, centers, others, live_count)
    depth, width = lax.axis_size("gz"), lax.axis_size("xy")
    chips = [
        [(2 * chip + core) * width + place for core in range(2) for place in range(width)]
        for chip in range(depth // 2)
    ]
    mid = lax.all_to_all(packed, ("gz", "xy"), 0, 0, tiled=True, axis_index_groups=chips)
    low = shift(mid, "gz", 2)
    high = shift(mid[..., :7, :], "gz", -2)
    return compute(low, mid, high, in_weight, env_weight, up_weight, out_weight.reshape(1, -1))


def solution(mesh):
    in_specs = (
        P(None, "gz", "xy", None),
        P("gz", "xy", None),
        P("gz", "xy", None),
        P("gz", "xy", None),
        P("gz", "xy"),
        P(),
        P(),
        P(),
        P(),
    )
    out_specs = (P("gz", "xy", None), P(None, "gz", "xy", None))
    return jax.shard_map(body, mesh=mesh, in_specs=in_specs, out_specs=out_specs, check_vma=False)
```

```python
import jax
import jax.numpy as jnp
from jax import lax
from jax.experimental import pallas as pl
from jax.experimental.pallas import tpu as pltpu
from jax.sharding import PartitionSpec as P

NB = 8
SPEC = 8
LAT = 128
CH = 32
SOFTEN = 0.01
CUTOFF = 3.5
COLS = 8
F32 = jnp.float32
BF16 = jnp.bfloat16
PI = 3.141592653589793


def halves(value):
    high = value.astype(BF16)
    low = (value - high.astype(F32)).astype(BF16)
    return high, low


def dot(left, right):
    return lax.dot_general(left, right, (((1,), (0,)), ((), ())), preferred_element_type=F32)


def dot_t(left, right):
    return lax.dot_general(left, right, (((1,), (1,)), ((), ())), preferred_element_type=F32)


def t_dot(left, right):
    return lax.dot_general(left, right, (((0,), (0,)), ((), ())), preferred_element_type=F32)


def both(value):
    return value[:, :128] + value[:, 128:]


def iota(shape, dim):
    return lax.broadcasted_iota(jnp.int32, shape, dim)


def flag(condition):
    return jnp.where(condition, 1.0, 0.0).astype(F32)


def kernel(
    far_ref, mid_ref, near_ref, in_ref, env_ref, up_ref, out_ref,
    energy_ref, force_ref,
    grid_s, rows_s, geo_s, w_first, w_env, w_env_t, w_up, w_down, w_rad, w_out,
    lat_s, slope_s, harm_s, msg_s, feat_s, dfeat_s, dlat_s, hout_s, back_s, vec_s,
    dfi_s, dfj_s, hot_c_s, hot_a_s, hot_at_s, index_s, weight_s,
):
    col0 = lax.axis_index("xy") * 2
    first_row = (lax.axis_index("gz") % 2) * 2 + 1

    lane = iota((128, 128), 1)
    sub = iota((128, 128), 0)
    w_in = in_ref[...]
    wr_hi, wr_lo = halves(w_in[0:8])
    wi_hi, wi_lo = halves(w_in[8:16])
    wj_hi, wj_lo = halves(w_in[16:24])
    lane8 = iota((8, 128), 1)
    sub8 = iota((8, 128), 0)
    spread = flag((lane8 // CH) == (sub8 % 4))
    first = jnp.concatenate(
        [x.astype(F32) for x in (wr_hi, wr_hi, wr_lo, wi_hi, wi_lo, wj_hi, wj_lo)], axis=0
    )
    w_first[:, 0:128] = jnp.concatenate([first, jnp.zeros((24, 128), F32)], axis=0).astype(BF16)
    w_first[:, 128:256] = jnp.concatenate(
        [jnp.zeros((56, 128), F32), spread, jnp.zeros((16, 128), F32)], axis=0
    ).astype(BF16)
    for block, table in enumerate(
        (
            flag(sub8 == 2),
            flag(sub8 == 3),
            flag(sub8 == 4),
            flag((sub8 == 5) | (sub8 == 6)),
        )
    ):
        w_first[:, 128 * block + 256 : 128 * block + 384] = jnp.concatenate(
            [jnp.zeros((64, 128), F32), table, jnp.zeros((8, 128), F32)], axis=0
        ).astype(BF16)
    env = env_ref[...]
    env_hi, env_lo = halves(env)
    tile = flag((iota((CH, 128), 1) % CH) == iota((CH, 128), 0)).astype(BF16)
    env4_hi = dot(env_hi, tile)
    env4_lo = dot(env_lo, tile)
    zero = jnp.zeros((128, 128), BF16)
    w_env[0:128, 0:128] = env4_hi.astype(BF16)
    w_env[0:128, 128:256] = env4_lo.astype(BF16)
    w_env[128:256, 0:128] = env4_hi.astype(BF16)
    w_env[128:256, 128:256] = zero
    env4_hi_t = jnp.transpose(env4_hi).astype(BF16)
    env4_lo_t = jnp.transpose(env4_lo).astype(BF16)
    w_env_t[0:128, 0:128] = env4_hi_t
    w_env_t[0:128, 128:256] = env4_lo_t
    w_env_t[128:256, 0:128] = env4_hi_t
    w_env_t[128:256, 128:256] = zero
    up = up_ref[...]
    up_l = up[0:128]
    up_p = jnp.concatenate([up[128:160]] * 4, axis=0)
    for base, block in ((0, up_l), (256, up_p)):
        hi, lo = halves(block)
        w_up[base : base + 128, 0:128] = hi
        w_up[base : base + 128, 128:256] = lo
        w_up[base + 128 : base + 256, 0:128] = hi
        w_up[base + 128 : base + 256, 128:256] = zero
        hi, lo = halves(jnp.transpose(block))
        w_down[0:128, base : base + 128] = hi
        w_down[128:256, base : base + 128] = hi
        w_down[0:128, base + 128 : base + 256] = lo
        w_down[128:256, base + 128 : base + 256] = zero
    z8 = jnp.zeros((8, 128), F32)
    wr_hi32 = wr_hi.astype(F32)
    wr_lo32 = wr_lo.astype(F32)
    ones4 = flag((lane8 // CH) == sub8)
    for block, parts in enumerate(
        ((wr_hi32, wr_lo32, z8, z8), (wr_hi32, z8, z8, z8), (z8, z8, ones4, z8), (z8, z8, ones4, z8))
    ):
        w_rad[:, 128 * block : 128 * block + 128] = jnp.concatenate(parts, axis=0).astype(BF16)
    out_row = out_ref[...]
    out_hi, out_lo = halves(out_row)
    out_hi32 = out_hi.astype(F32)
    out_lo32 = out_lo.astype(F32)
    z1 = jnp.zeros((1, 128), F32)
    pad14 = jnp.zeros((14, 128), F32)
    w_out[:, 0:128] = jnp.concatenate([out_hi32, out_lo32, pad14], axis=0).astype(BF16)
    w_out[:, 128:256] = jnp.concatenate([out_hi32, z1, pad14], axis=0).astype(BF16)

    odd = (lax.axis_index("gz") // 2) % 2
    for source, start in ((far_ref, 8 * odd), (mid_ref, 4), (near_ref, 8 - 8 * odd)):
        for peer in range(8):
            for row in range(2):
                for col in range(2):
                    place = start * (COLS * 8) + ((peer // 4 * 2 + row) * COLS + peer % 4 * 2 + col) * 8
                    size = source.shape[3]
                    grid_s[pl.ds(pl.multiple_of(place, 8), size), :] = source[peer, row, col]

    def quantity(row, which):
        return grid_s[pl.ds((first_row + row) * 64 + which, 8, stride=8), :]

    tables = [[quantity(row, which) for which in range(4)] for row in range(8)]
    for f in range(6):
        center = quantity(f + 1, 4)
        other = quantity(f + 1, 5)
        count = quantity(f + 1, 6)
        center_i = center.astype(jnp.int32)
        other_i = other.astype(jnp.int32)
        place = other_i // 128
        atom = other_i % 128
        at_i = [jnp.take_along_axis(tables[f + 1][which], center_i, axis=1) for which in range(4)]
        at_j = [jnp.zeros((8, 128), F32) for _ in range(4)]
        for offset in range(9):
            dr, dc = offset // 3 - 1, offset % 3 - 1
            here = place == offset
            for which in range(4):
                table = tables[f + 1 + dr][which]
                if dc:
                    table = pltpu.roll(table, (-dc) % 8, 0)
                value = jnp.take_along_axis(table, atom, axis=1)
                if which == 0:
                    value = value + float(dr)
                if which == 1:
                    value = value + float(dc)
                at_j[which] = jnp.where(here, value, at_j[which])
        dz, dx, dy = (at_j[which] - at_i[which] for which in range(3))
        distance = jnp.sqrt(dz * dz + dx * dx + dy * dy + SOFTEN)
        inverse = 1.0 / distance
        scaled = distance * (1.0 / CUTOFF)
        inner = 1.0 - scaled * scaled
        envelope = inner * inner
        slope = (-4.0 / CUTOFF) * inner * scaled
        live = flag(iota((8, 128), 1).astype(F32) < count)
        angle = PI * scaled
        sine, cosine = jnp.sin(angle), jnp.cos(angle)
        base = f * COLS * 32

        def put(which, value):
            rows_s[pl.ds(base + which, 8, stride=32), :] = value

        def split_put(which, gap, value):
            high = value.astype(BF16).astype(F32)
            put(which, high)
            put(which + gap, value - high)

        s_old, s_now = jnp.zeros_like(sine), sine
        c_old, c_now = jnp.ones_like(sine), cosine
        scale = inverse * envelope
        slope_scale = inverse * slope - inverse * scale
        for k in range(1, NB + 1):
            split_put(k - 1, 8, s_now * scale)
            geo_s[f, k - 1] = (k * PI / CUTOFF) * c_now * scale + s_now * slope_scale
            s_old, s_now = s_now, 2.0 * cosine * s_now - s_old
            c_old, c_now = c_now, 2.0 * cosine * c_now - c_old
        for m, value in enumerate((live, live * dz * inverse, live * dx * inverse, live * dy * inverse)):
            split_put(16 + m, 4, value)
        put(24, at_i[3])
        put(25, at_j[3])
        put(26, center)
        put(27, atom.astype(F32))
        put(28, place.astype(F32))
        split_put(29, 1, envelope * live)
        put(31, live)
        for which, value in enumerate((dz, dx, dy, inverse, live, slope, envelope)):
            geo_s[f, 8 + which] = value

    def slot(f, i):
        return f * COLS + ((col0 + (i + COLS - 2)) & (COLS - 1))

    def bin_rows(f, i, first, size):
        return rows_s[pl.ds(slot(f, i) * 32 + first, size), :]

    lanes = iota((128, 128), 1).astype(F32).astype(BF16)
    subs = iota((128, 128), 0).astype(F32).astype(BF16)
    one = jnp.ones((128, 128), BF16)

    def hot_rows(row):
        wide = jnp.broadcast_to(row, (128, 128)).astype(BF16)
        return jnp.where(wide == subs, one, zero)

    def feature_group(f, cols):
        inputs = []
        for i in cols:
            rows = bin_rows(f, i, 0, 32)
            spec_i = flag(rows[24:25] == iota((8, 128), 0).astype(F32))
            spec_j = flag(rows[25:26] == iota((8, 128), 0).astype(F32))
            inputs.append(jnp.concatenate(
                [rows[0:16], rows[0:8], spec_i, spec_i, spec_j, spec_j, rows[16:32], jnp.zeros((8, 128), F32)],
                axis=0,
            ).astype(BF16))
        mixed = t_dot(jnp.concatenate(inputs, axis=1), w_first[...])
        pre, harm = mixed[:, :128], mixed[:, 128:256]
        narrow = mixed[:, 256:640].astype(BF16)
        gate = 0.5 + 0.5 * jnp.tanh(0.5 * pre)
        latent = pre * gate
        lat = jnp.concatenate(halves(latent), axis=1)
        weights = both(dot(lat, w_env[...]))
        slope = gate + latent * (1.0 - gate)
        high, low = halves(weights * harm)
        for n, i in enumerate(cols):
            part = slice(128 * n, 128 * n + 128)
            message = jnp.concatenate([high[part], low[part]], axis=0)
            hot = hot_rows(bin_rows(f, i, 26, 1))
            feat = dot(jnp.concatenate([hot, hot], axis=1), message)
            lat_s[f, i] = lat[part]
            index_s[f, i] = narrow[part]
            weight_s[f, i] = mixed[part, 640:]
            feat_s[f, i] = feat.astype(BF16)
            if 1 <= i <= 4:
                slope_s[f, i - 1] = slope[part]
                harm_s[f, i - 1] = harm[part]
                msg_s[f, i - 1] = weights[part]

    def feature_step(f, carry):
        for group in FEATURE_GROUPS:
            feature_group(f, group)
        return carry

    for f in range(6):
        feature_step(f, 0)

    def energy_group(f, cols, reach, inside_row):
        feat_i, feat_j, weight, hots = [], [], [], []
        for i in cols:
            inside = inside_row and 1 <= i <= 4
            narrow = index_s[f, i]
            center, atom, place = narrow[:, :128], narrow[:, 128:256], narrow[:, 256:]
            weight.append(weight_s[f, i])
            hot_c = jnp.where(center == lanes, one, zero)
            hot_a = jnp.where(atom == lanes, one, zero)
            feat_i.append(dot(hot_c, feat_s[f, i]))
            columns, tables_j = [], []
            for target, code in reach:
                for dc in (-1, 0, 1):
                    if inside or 1 <= i + dc <= 4:
                        columns.append(jnp.where(place == jnp.asarray(code + (dc + 1), F32).astype(BF16), hot_a, zero))
                        tables_j.append(feat_s[target, i + dc])
            feat_j.append(dot(jnp.concatenate(columns, axis=1), jnp.concatenate(tables_j, axis=0)))
            hots.append(hot_c)
            if inside:
                hot_c_s[f, i - 1] = hot_c
                hot_a_s[f, i - 1] = hot_a
            hot_at_s[f, i] = hot_rows(bin_rows(f, i, 27, 1))
        feat_i = jnp.concatenate(feat_i, axis=0)
        feat_j = jnp.concatenate(feat_j, axis=0)
        weight = jnp.concatenate(weight, axis=0)
        lat = jnp.concatenate([lat_s[f, i] for i in cols], axis=0)
        prod = jnp.concatenate(halves(feat_i * feat_j), axis=1)
        pre = both(dot(jnp.concatenate([lat, prod], axis=1), w_up[...]))
        gate = 0.5 + 0.5 * jnp.tanh(0.5 * pre)
        hidden = pre * gate
        d_pre = out_ref[...] * (gate + hidden * (1.0 - gate)) * weight
        d_pre = jnp.concatenate(halves(d_pre), axis=1)
        within = inside_row and 1 <= cols[0] <= 4
        if within:
            down = dot(d_pre, w_down[...])
            d_lat = both(down[:, :256])
            d_prod = both(down[:, 256:])
            hid = jnp.concatenate(halves(hidden), axis=1)
            readout = dot_t(w_out[...], hid)
            d_i = jnp.concatenate(halves(d_prod * feat_j), axis=1)
        else:
            d_prod = both(dot(d_pre, w_down[:, 256:]))
        d_j = jnp.concatenate(halves(d_prod * feat_i), axis=1)
        for n, i in enumerate(cols):
            part = slice(128 * n, 128 * n + 128)
            dfj_s[f, i] = d_j[part]
            if within:
                dfi_s[f, i - 1] = d_i[part]
                dlat_s[f, i - 1] = d_lat[part]
                value = readout[0:1, part] + readout[1:2, part]
                hout_s[pl.ds((f * 4 + (i - 1)) * 8, 8), :] = jnp.broadcast_to(value, (8, 128))
                if i in (2, 3):
                    rows = bin_rows(f, i, 24, 8)
                    edge = value * (rows[5:6] + rows[6:7])
                    high = edge.astype(BF16).astype(F32)
                    parts = jnp.concatenate([high, edge - high, jnp.zeros((14, 128), F32)], axis=0)
                    summed = dot(parts.astype(BF16), hots[n])
                    energy_ref[jnp.clip(f - 2, 0, 1), pl.ds(i - 2, 1), :] = jnp.where(
                        (f == 2) | (f == 3), summed[0:1] + summed[1:2],
                        energy_ref[jnp.clip(f - 2, 0, 1), pl.ds(i - 2, 1), :])

    def energy_step(f, carry):
        reach = [(f + dr, 3.0 * (dr + 1)) for dr in (-1, 0, 1)]
        for group in ENERGY_GROUPS:
            energy_group(f, group, reach, True)
        return carry

    def rim_step(t, carry):
        for group in RIM_GROUPS:
            energy_group(5 * t, group, [(1 + 3 * t, 6.0 - 6.0 * t.astype(F32))], False)
        return carry

    energy_ref[...] = jnp.zeros_like(energy_ref)
    for f in range(1, 5):
        energy_step(f, 0)
    lax.fori_loop(0, 2, rim_step, 0)

    def backward_group(f, cols):
        d_msg = []
        for i in cols:
            columns, terms = [hot_rows(bin_rows(f, i, 26, 1))], [dfi_s[f, i - 1]]
            for dr in (-1, 0, 1):
                for dc in (-1, 0, 1):
                    code = float(3 * (1 - dr) + (1 - dc))
                    mask = flag(bin_rows(f + dr, i + dc, 28, 1) == code)
                    mask = jnp.broadcast_to(mask, (128, 128)).astype(BF16)
                    columns.append(hot_at_s[f + dr, i + dc] * mask)
                    terms.append(dfj_s[f + dr, i + dc])
            d_feat = both(dot(jnp.concatenate(columns, axis=1), jnp.concatenate(terms, axis=0)))
            hot = hot_c_s[f, i - 1]
            d_msg.append(dot(jnp.concatenate([hot, hot], axis=1), jnp.concatenate(halves(d_feat), axis=0)))
        d_msg = jnp.concatenate(d_msg, axis=0)
        gather = lambda ref: jnp.concatenate([ref[f, i - 1] for i in cols], axis=0)
        d_weight = jnp.concatenate(halves(d_msg * gather(harm_s)), axis=1)
        d_lat = both(dot(d_weight, w_env_t[...])) + gather(dlat_s)
        d_pre = jnp.concatenate(
            halves(d_lat * gather(slope_s)) + halves(d_msg * gather(msg_s)), axis=1
        )
        rows = dot_t(w_rad[...], d_pre)
        result = jnp.concatenate([rows[0:8] + rows[8:16], rows[16:24]], axis=0)
        for n, i in enumerate(cols):
            back_s[pl.ds(slot(f, i) * 16, 16), :] = result[:, 128 * n : 128 * n + 128]

    def backward_step(f, carry):
        for group in BACK_GROUPS:
            backward_group(f, group)
        return carry

    back_s[...] = jnp.zeros_like(back_s)
    for f in range(1, 5):
        backward_step(f, 0)

    for f in range(1, 5):
        def got(which):
            return back_s[pl.ds(f * COLS * 16 + which, 8, stride=16), :]

        dz, dx, dy, inverse, live, slope = (geo_s[f, 8 + which] for which in range(6))
        d_dist = jnp.zeros((8, 128), F32)
        for k in range(NB):
            d_dist = d_dist + got(k) * geo_s[f, k]
        readout = jnp.zeros((8, 128), F32)
        col = iota((8, 128), 0)
        for i in range(1, 5):
            value = hout_s[(f * 4 + i - 1) * 8 : (f * 4 + i - 1) * 8 + 8, :]
            readout = jnp.where(col == ((col0 + (i + COLS - 2)) & (COLS - 1)), value, readout)
        d_dist = d_dist + readout * live * slope
        hz, hx, hy = (got(8 + m) * live for m in (1, 2, 3))
        d_dist = d_dist - (hz * dz + hx * dx + hy * dy) * inverse * inverse
        along = d_dist * inverse
        for axis, (delta, own) in enumerate(((dz, hz), (dx, hx), (dy, hy))):
            value = along * delta + own * inverse
            high = value.astype(BF16).astype(F32)
            vec_s[pl.ds(f * COLS * 8 + 2 * axis, 8, stride=8), :] = high
            vec_s[pl.ds(f * COLS * 8 + 2 * axis + 1, 8, stride=8), :] = value - high
        for spare in (6, 7):
            vec_s[pl.ds(f * COLS * 8 + spare, 8, stride=8), :] = jnp.zeros((8, 128), F32)

    total = [[jnp.zeros((8, 128), F32) for _ in range(2)] for _ in range(2)]
    for f in range(1, 5):
        for i in range(1, 5):
            vec = vec_s[pl.ds(slot(f, i) * 8, 8), :]
            place = bin_rows(f, i, 28, 1)
            targets = [(dr, dc) for dr in (-1, 0, 1) for dc in (-1, 0, 1) if 2 <= i + dc <= 3 and 2 <= f + dr <= 3]
            parts = [vec * flag(place == float((dr + 1) * 3 + dc + 1)) for dr, dc in targets]
            if len(parts) % 2:
                parts.append(jnp.zeros((8, 128), F32))
            moved = dot(jnp.concatenate(parts, axis=0).astype(BF16), hot_a_s[f, i - 1])
            for index, (dr, dc) in enumerate(targets):
                total[f + dr - 2][i + dc - 2] -= moved[8 * index : 8 * index + 8]
            if i in (2, 3) and f in (2, 3):
                centered = jnp.concatenate([vec, jnp.zeros((8, 128), F32)], axis=0).astype(BF16)
                total[f - 2][i - 2] += dot(centered, hot_c_s[f, i - 1])[0:8]
    for row in range(2):
        for col in range(2):
            value = total[row][col]
            for axis in range(3):
                force_ref[axis, row, pl.ds(col, 1), :] = (
                    value[2 * axis : 2 * axis + 1] + value[2 * axis + 1 : 2 * axis + 2]
                )


FEATURE_GROUPS = ((0, 1, 2, 3, 4, 5),)
ENERGY_GROUPS = ((0, 5), (1, 2, 3, 4))
RIM_GROUPS = ((0, 1, 2, 3, 4, 5),)
BACK_GROUPS = ((1, 2, 3, 4),)


def compute(far, mid, near, in_weight, env_weight, up_weight, out_weight):
    return pl.pallas_call(
        kernel,
        out_shape=(
            jax.ShapeDtypeStruct((2, 2, 128), F32),
            jax.ShapeDtypeStruct((3, 2, 2, 128), F32),
        ),
        in_specs=[pl.BlockSpec(memory_space=pltpu.VMEM)] * 7,
        out_specs=[pl.BlockSpec(memory_space=pltpu.VMEM)] * 2,
        scratch_shapes=[
            pltpu.VMEM((12 * COLS * 8, 128), F32),
            pltpu.VMEM((6 * COLS * 32, 128), F32),
            pltpu.VMEM((6, 16, COLS, 128), F32),
            pltpu.VMEM((80, 768), BF16),
            pltpu.VMEM((256, 256), BF16),
            pltpu.VMEM((256, 256), BF16),
            pltpu.VMEM((512, 256), BF16),
            pltpu.VMEM((256, 512), BF16),
            pltpu.VMEM((32, 512), BF16),
            pltpu.VMEM((16, 256), BF16),
            pltpu.VMEM((6, 6, 128, 256), BF16),
            pltpu.VMEM((6, 4, 128, 128), F32),
            pltpu.VMEM((6, 4, 128, 128), F32),
            pltpu.VMEM((6, 4, 128, 128), F32),
            pltpu.VMEM((6, 6, 128, 128), BF16),
            pltpu.VMEM((8, 128), F32),
            pltpu.VMEM((6, 4, 128, 128), F32),
            pltpu.VMEM((6 * 4 * 8, 128), F32),
            pltpu.VMEM((6 * COLS * 16, 128), F32),
            pltpu.VMEM((6 * COLS * 8, 128), F32),
            pltpu.VMEM((6, 4, 128, 256), BF16),
            pltpu.VMEM((6, 6, 128, 256), BF16),
            pltpu.VMEM((6, 4, 128, 128), BF16),
            pltpu.VMEM((6, 4, 128, 128), BF16),
            pltpu.VMEM((6, 6, 128, 128), BF16),
            pltpu.VMEM((6, 6, 128, 384), BF16),
            pltpu.VMEM((6, 6, 128, 128), F32),
        ],
        compiler_params=pltpu.CompilerParams(vmem_limit_bytes=40 * 1024 * 1024),
        name="potential",
    )(far, mid, near, in_weight, env_weight, up_weight, out_weight)


def pack_kernel(coords_ref, species_ref, centers_ref, others_ref, live_ref, packed_ref):
    for row in range(2):
        for col in range(2):
            at = pl.ds(col, 1)
            tile = jnp.concatenate(
                [coords_ref[axis, row, at, :] for axis in range(3)]
                + [ref[row, at, :].astype(F32) for ref in (species_ref, centers_ref, others_ref)]
                + [jnp.full((1, 128), live_ref[row, col], jnp.int32).astype(F32), jnp.zeros((1, 128), F32)],
                axis=0,
            )
            for peer in range(8):
                packed_ref[peer, row, col] = tile


def pack(coords, species, centers, others, live_count):
    return pl.pallas_call(
        pack_kernel,
        out_shape=jax.ShapeDtypeStruct((8, 2, 2, 8, 128), F32),
        in_specs=[pl.BlockSpec(memory_space=pltpu.VMEM)] * 4 + [pl.BlockSpec(memory_space=pltpu.SMEM)],
        out_specs=pl.BlockSpec(memory_space=pltpu.VMEM),
        name="pack",
    )(coords, species, centers, others, live_count)


def swap(value, count, first):
    return lax.ppermute(value, "gz", [(i, (((i + first) ^ 2) - first) % count) for i in range(count)])


def body(
    coords, species, centers, others, live_count, in_weight, env_weight, up_weight, out_weight
):
    packed = pack(coords, species, centers, others, live_count)
    depth, width = lax.axis_size("gz"), lax.axis_size("xy")
    chips = [
        [(2 * chip + core) * width + place for core in range(2) for place in range(width)]
        for chip in range(depth // 2)
    ]
    mid = lax.all_to_all(packed, ("gz", "xy"), 0, 0, tiled=True, axis_index_groups=chips)
    far = swap(mid, depth, 2)
    near = swap(mid[..., :7, :], depth, 0)
    return compute(far, mid, near, in_weight, env_weight, up_weight, out_weight.reshape(1, -1))


def solution(mesh):
    in_specs = (
        P(None, "gz", "xy", None),
        P("gz", "xy", None),
        P("gz", "xy", None),
        P("gz", "xy", None),
        P("gz", "xy"),
        P(),
        P(),
        P(),
        P(),
    )
    out_specs = (P("gz", "xy", None), P(None, "gz", "xy", None))
    return jax.shard_map(body, mesh=mesh, in_specs=in_specs, out_specs=out_specs, check_vma=False)
```

```python
import jax
import jax.numpy as jnp
from jax import lax
from jax.experimental import pallas as pl
from jax.experimental.pallas import tpu as pltpu
from jax.sharding import PartitionSpec as P

NB = 8
SPEC = 8
LAT = 128
CH = 32
SOFTEN = 0.01
CUTOFF = 3.5
COLS = 8
F32 = jnp.float32
BF16 = jnp.bfloat16
PI = 3.141592653589793


def halves(value):
    high = value.astype(BF16)
    low = (value - high.astype(F32)).astype(BF16)
    return high, low


def dot(left, right):
    return lax.dot_general(left, right, (((1,), (0,)), ((), ())), preferred_element_type=F32)


def dot_t(left, right):
    return lax.dot_general(left, right, (((1,), (1,)), ((), ())), preferred_element_type=F32)


def t_dot(left, right):
    return lax.dot_general(left, right, (((0,), (0,)), ((), ())), preferred_element_type=F32)


def both(value):
    return value[:, :128] + value[:, 128:]


def iota(shape, dim):
    return lax.broadcasted_iota(jnp.int32, shape, dim)


def flag(condition):
    return jnp.where(condition, 1.0, 0.0).astype(F32)


def kernel(
    far_ref, mid_ref, near_ref, in_ref, env_ref, up_ref, out_ref,
    energy_ref, force_ref,
    grid_s, rows_s, geo_s, w_first, w_env, w_env_t, w_up, w_down, w_rad, w_out,
    lat_s, slope_s, harm_s, msg_s, feat_s, dfeat_s, dlat_s, hout_s, back_s, vec_s,
    dfi_s, dfj_s, hot_c_s, hot_a_s, hot_at_s, index_s, weight_s,
):
    col0 = lax.axis_index("xy") * 2
    first_row = (lax.axis_index("gz") % 2) * 2 + 1

    lane = iota((128, 128), 1)
    sub = iota((128, 128), 0)
    w_in = in_ref[...]
    wr_hi, wr_lo = halves(w_in[0:8])
    wi_hi, wi_lo = halves(w_in[8:16])
    wj_hi, wj_lo = halves(w_in[16:24])
    lane8 = iota((8, 128), 1)
    sub8 = iota((8, 128), 0)
    spread = flag((lane8 // CH) == (sub8 % 4))
    first = jnp.concatenate(
        [x.astype(F32) for x in (wr_hi, wr_hi, wr_lo, wi_hi, wi_lo, wj_hi, wj_lo)], axis=0
    )
    w_first[:, 0:128] = jnp.concatenate([first, jnp.zeros((24, 128), F32)], axis=0).astype(BF16)
    w_first[:, 128:256] = jnp.concatenate(
        [jnp.zeros((56, 128), F32), spread, jnp.zeros((16, 128), F32)], axis=0
    ).astype(BF16)
    for block, table in enumerate(
        (
            flag(sub8 == 2),
            flag(sub8 == 3),
            flag(sub8 == 4),
            flag((sub8 == 5) | (sub8 == 6)),
        )
    ):
        w_first[:, 128 * block + 256 : 128 * block + 384] = jnp.concatenate(
            [jnp.zeros((64, 128), F32), table, jnp.zeros((8, 128), F32)], axis=0
        ).astype(BF16)
    env = env_ref[...]
    env_hi, env_lo = halves(env)
    tile = flag((iota((CH, 128), 1) % CH) == iota((CH, 128), 0)).astype(BF16)
    env4_hi = dot(env_hi, tile)
    env4_lo = dot(env_lo, tile)
    zero = jnp.zeros((128, 128), BF16)
    w_env[0:128, 0:128] = env4_hi.astype(BF16)
    w_env[0:128, 128:256] = env4_lo.astype(BF16)
    w_env[128:256, 0:128] = env4_hi.astype(BF16)
    w_env[128:256, 128:256] = zero
    env4_hi_t = jnp.transpose(env4_hi).astype(BF16)
    env4_lo_t = jnp.transpose(env4_lo).astype(BF16)
    w_env_t[0:128, 0:128] = env4_hi_t
    w_env_t[0:128, 128:256] = env4_lo_t
    w_env_t[128:256, 0:128] = env4_hi_t
    w_env_t[128:256, 128:256] = zero
    up = up_ref[...]
    up_l = up[0:128]
    up_p = jnp.concatenate([up[128:160]] * 4, axis=0)
    for base, block in ((0, up_l), (256, up_p)):
        hi, lo = halves(block)
        w_up[base : base + 128, 0:128] = hi
        w_up[base : base + 128, 128:256] = lo
        w_up[base + 128 : base + 256, 0:128] = hi
        w_up[base + 128 : base + 256, 128:256] = zero
        hi, lo = halves(jnp.transpose(block))
        w_down[0:128, base : base + 128] = hi
        w_down[128:256, base : base + 128] = hi
        w_down[0:128, base + 128 : base + 256] = lo
        w_down[128:256, base + 128 : base + 256] = zero
    z8 = jnp.zeros((8, 128), F32)
    wr_hi32 = wr_hi.astype(F32)
    wr_lo32 = wr_lo.astype(F32)
    ones4 = flag((lane8 // CH) == sub8)
    for block, parts in enumerate(
        ((wr_hi32, wr_lo32, z8, z8), (wr_hi32, z8, z8, z8), (z8, z8, ones4, z8), (z8, z8, ones4, z8))
    ):
        w_rad[:, 128 * block : 128 * block + 128] = jnp.concatenate(parts, axis=0).astype(BF16)
    out_row = out_ref[...]
    out_hi, out_lo = halves(out_row)
    out_hi32 = out_hi.astype(F32)
    out_lo32 = out_lo.astype(F32)
    z1 = jnp.zeros((1, 128), F32)
    pad14 = jnp.zeros((14, 128), F32)
    w_out[:, 0:128] = jnp.concatenate([out_hi32, out_lo32, pad14], axis=0).astype(BF16)
    w_out[:, 128:256] = jnp.concatenate([out_hi32, z1, pad14], axis=0).astype(BF16)

    odd = (lax.axis_index("gz") // 2) % 2
    for source, start in ((far_ref, 8 * odd), (mid_ref, 4), (near_ref, 8 - 8 * odd)):
        for peer in range(8):
            for row in range(2):
                for col in range(2):
                    place = start * (COLS * 8) + ((peer // 4 * 2 + row) * COLS + peer % 4 * 2 + col) * 8
                    size = source.shape[3]
                    grid_s[pl.ds(pl.multiple_of(place, 8), size), :] = source[peer, row, col]

    def quantity(row, which):
        return grid_s[pl.ds((first_row + row) * 64 + which, 8, stride=8), :]

    tables = [[quantity(row, which) for which in range(4)] for row in range(8)]
    for f in range(6):
        center = quantity(f + 1, 4)
        other = quantity(f + 1, 5)
        count = quantity(f + 1, 6)
        center_i = center.astype(jnp.int32)
        other_i = other.astype(jnp.int32)
        place = other_i // 128
        atom = other_i % 128
        at_i = [jnp.take_along_axis(tables[f + 1][which], center_i, axis=1) for which in range(4)]
        at_j = [jnp.zeros((8, 128), F32) for _ in range(4)]
        for offset in range(9):
            dr, dc = offset // 3 - 1, offset % 3 - 1
            here = place == offset
            for which in range(4):
                table = tables[f + 1 + dr][which]
                if dc:
                    table = pltpu.roll(table, (-dc) % 8, 0)
                value = jnp.take_along_axis(table, atom, axis=1)
                if which == 0:
                    value = value + float(dr)
                if which == 1:
                    value = value + float(dc)
                at_j[which] = jnp.where(here, value, at_j[which])
        dz, dx, dy = (at_j[which] - at_i[which] for which in range(3))
        distance = jnp.sqrt(dz * dz + dx * dx + dy * dy + SOFTEN)
        inverse = 1.0 / distance
        scaled = distance * (1.0 / CUTOFF)
        inner = 1.0 - scaled * scaled
        envelope = inner * inner
        slope = (-4.0 / CUTOFF) * inner * scaled
        live = flag(iota((8, 128), 1).astype(F32) < count)
        angle = PI * scaled
        sine, cosine = jnp.sin(angle), jnp.cos(angle)
        base = f * COLS * 32

        def put(which, value):
            rows_s[pl.ds(base + which, 8, stride=32), :] = value

        def split_put(which, gap, value):
            high = value.astype(BF16).astype(F32)
            put(which, high)
            put(which + gap, value - high)

        s_old, s_now = jnp.zeros_like(sine), sine
        c_old, c_now = jnp.ones_like(sine), cosine
        scale = inverse * envelope
        slope_scale = inverse * slope - inverse * scale
        for k in range(1, NB + 1):
            split_put(k - 1, 8, s_now * scale)
            geo_s[f, k - 1] = (k * PI / CUTOFF) * c_now * scale + s_now * slope_scale
            s_old, s_now = s_now, 2.0 * cosine * s_now - s_old
            c_old, c_now = c_now, 2.0 * cosine * c_now - c_old
        for m, value in enumerate((live, live * dz * inverse, live * dx * inverse, live * dy * inverse)):
            split_put(16 + m, 4, value)
        put(24, at_i[3])
        put(25, at_j[3])
        put(26, center)
        put(27, atom.astype(F32))
        put(28, place.astype(F32))
        split_put(29, 1, envelope * live)
        put(31, live)
        for which, value in enumerate((dz, dx, dy, inverse, live, slope, envelope)):
            geo_s[f, 8 + which] = value

    def slot(f, i):
        return f * COLS + ((col0 + (i + COLS - 2)) & (COLS - 1))

    def bin_rows(f, i, first, size):
        return rows_s[pl.ds(slot(f, i) * 32 + first, size), :]

    lanes = iota((128, 128), 1).astype(F32).astype(BF16)
    subs = iota((128, 128), 0).astype(F32).astype(BF16)
    one = jnp.ones((128, 128), BF16)

    def hot_rows(row):
        wide = jnp.broadcast_to(row, (128, 128)).astype(BF16)
        return jnp.where(wide == subs, one, zero)

    def feature_group(f, cols):
        inputs = []
        for i in cols:
            rows = bin_rows(f, i, 0, 32)
            spec_i = flag(rows[24:25] == iota((8, 128), 0).astype(F32))
            spec_j = flag(rows[25:26] == iota((8, 128), 0).astype(F32))
            inputs.append(jnp.concatenate(
                [rows[0:16], rows[0:8], spec_i, spec_i, spec_j, spec_j, rows[16:32], jnp.zeros((8, 128), F32)],
                axis=0,
            ).astype(BF16))
        mixed = t_dot(jnp.concatenate(inputs, axis=1), w_first[...])
        pre, harm = mixed[:, :128], mixed[:, 128:256]
        narrow = mixed[:, 256:640].astype(BF16)
        gate = 0.5 + 0.5 * jnp.tanh(0.5 * pre)
        latent = pre * gate
        lat = jnp.concatenate(halves(latent), axis=1)
        weights = both(dot(lat, w_env[...]))
        slope = gate + latent * (1.0 - gate)
        high, low = halves(weights * harm)
        for n, i in enumerate(cols):
            part = slice(128 * n, 128 * n + 128)
            message = jnp.concatenate([high[part], low[part]], axis=0)
            hot = hot_rows(bin_rows(f, i, 26, 1))
            feat = dot(jnp.concatenate([hot, hot], axis=1), message)
            lat_s[f, i] = lat[part]
            index_s[f, i] = narrow[part]
            weight_s[f, i] = mixed[part, 640:]
            feat_s[f, i] = feat.astype(BF16)
            if 1 <= i <= 4:
                slope_s[f, i - 1] = slope[part]
                harm_s[f, i - 1] = harm[part]
                msg_s[f, i - 1] = weights[part]

    def feature_step(f, carry):
        for group in FEATURE_GROUPS:
            feature_group(f, group)
        return carry

    for f in range(6):
        feature_step(f, 0)

    def energy_group(f, cols, reach, inside_row):
        feat_i, feat_j, weight, hots = [], [], [], []
        for i in cols:
            inside = inside_row and 1 <= i <= 4
            narrow = index_s[f, i]
            center, atom, place = narrow[:, :128], narrow[:, 128:256], narrow[:, 256:]
            weight.append(weight_s[f, i])
            hot_c = jnp.where(center == lanes, one, zero)
            hot_a = jnp.where(atom == lanes, one, zero)
            feat_i.append(dot(hot_c, feat_s[f, i]))
            columns, tables_j = [], []
            for target, code in reach:
                for dc in (-1, 0, 1):
                    if inside or 1 <= i + dc <= 4:
                        columns.append(jnp.where(place == jnp.asarray(code + (dc + 1), F32).astype(BF16), hot_a, zero))
                        tables_j.append(feat_s[target, i + dc])
            feat_j.append(dot(jnp.concatenate(columns, axis=1), jnp.concatenate(tables_j, axis=0)))
            hots.append(hot_c)
            if inside:
                hot_c_s[f, i - 1] = hot_c
                hot_a_s[f, i - 1] = hot_a
            hot_at_s[f, i] = hot_rows(bin_rows(f, i, 27, 1))
        feat_i = jnp.concatenate(feat_i, axis=0)
        feat_j = jnp.concatenate(feat_j, axis=0)
        weight = jnp.concatenate(weight, axis=0)
        lat = jnp.concatenate([lat_s[f, i] for i in cols], axis=0)
        prod = jnp.concatenate(halves(feat_i * feat_j), axis=1)
        pre = both(dot(jnp.concatenate([lat, prod], axis=1), w_up[...]))
        gate = 0.5 + 0.5 * jnp.tanh(0.5 * pre)
        hidden = pre * gate
        d_pre = out_ref[...] * (gate + hidden * (1.0 - gate)) * weight
        d_pre = jnp.concatenate(halves(d_pre), axis=1)
        within = inside_row and 1 <= cols[0] <= 4
        if within:
            down = dot(d_pre, w_down[...])
            d_lat = both(down[:, :256])
            d_prod = both(down[:, 256:])
            hid = jnp.concatenate(halves(hidden), axis=1)
            readout = dot_t(w_out[...], hid)
            d_i = jnp.concatenate(halves(d_prod * feat_j), axis=1)
        else:
            d_prod = both(dot(d_pre, w_down[:, 256:]))
        d_j = jnp.concatenate(halves(d_prod * feat_i), axis=1)
        for n, i in enumerate(cols):
            part = slice(128 * n, 128 * n + 128)
            dfj_s[f, i] = d_j[part]
            if within:
                dfi_s[f, i - 1] = d_i[part]
                dlat_s[f, i - 1] = d_lat[part]
                value = readout[0:1, part] + readout[1:2, part]
                hout_s[pl.ds((f * 4 + (i - 1)) * 8, 8), :] = jnp.broadcast_to(value, (8, 128))
                if i in (2, 3):
                    rows = bin_rows(f, i, 24, 8)
                    edge = value * (rows[5:6] + rows[6:7])
                    high = edge.astype(BF16).astype(F32)
                    parts = jnp.concatenate([high, edge - high, jnp.zeros((14, 128), F32)], axis=0)
                    summed = dot(parts.astype(BF16), hots[n])
                    energy_ref[jnp.clip(f - 2, 0, 1), pl.ds(i - 2, 1), :] = jnp.where(
                        (f == 2) | (f == 3), summed[0:1] + summed[1:2],
                        energy_ref[jnp.clip(f - 2, 0, 1), pl.ds(i - 2, 1), :])

    def energy_step(f, carry):
        reach = [(f + dr, 3.0 * (dr + 1)) for dr in (-1, 0, 1)]
        for group in ENERGY_GROUPS:
            energy_group(f, group, reach, True)
        return carry

    def rim_step(t, carry):
        for group in RIM_GROUPS:
            energy_group(5 * t, group, [(1 + 3 * t, 6.0 - 6.0 * t.astype(F32))], False)
        return carry

    energy_ref[...] = jnp.zeros_like(energy_ref)
    for f in range(1, 5):
        energy_step(f, 0)
    lax.fori_loop(0, 2, rim_step, 0)

    def backward_group(f, cols):
        d_msg = []
        for i in cols:
            columns, terms = [hot_rows(bin_rows(f, i, 26, 1))], [dfi_s[f, i - 1]]
            for dr in (-1, 0, 1):
                for dc in (-1, 0, 1):
                    code = float(3 * (1 - dr) + (1 - dc))
                    mask = flag(bin_rows(f + dr, i + dc, 28, 1) == code)
                    mask = jnp.broadcast_to(mask, (128, 128)).astype(BF16)
                    columns.append(hot_at_s[f + dr, i + dc] * mask)
                    terms.append(dfj_s[f + dr, i + dc])
            d_feat = both(dot(jnp.concatenate(columns, axis=1), jnp.concatenate(terms, axis=0)))
            hot = hot_c_s[f, i - 1]
            d_msg.append(dot(jnp.concatenate([hot, hot], axis=1), jnp.concatenate(halves(d_feat), axis=0)))
        d_msg = jnp.concatenate(d_msg, axis=0)
        gather = lambda ref: jnp.concatenate([ref[f, i - 1] for i in cols], axis=0)
        d_weight = jnp.concatenate(halves(d_msg * gather(harm_s)), axis=1)
        d_lat = both(dot(d_weight, w_env_t[...])) + gather(dlat_s)
        d_pre = jnp.concatenate(
            halves(d_lat * gather(slope_s)) + halves(d_msg * gather(msg_s)), axis=1
        )
        rows = dot_t(w_rad[...], d_pre)
        result = jnp.concatenate([rows[0:8] + rows[8:16], rows[16:24]], axis=0)
        for n, i in enumerate(cols):
            back_s[pl.ds(slot(f, i) * 16, 16), :] = result[:, 128 * n : 128 * n + 128]

    def backward_step(f, carry):
        for group in BACK_GROUPS:
            backward_group(f, group)
        return carry

    back_s[...] = jnp.zeros_like(back_s)
    for f in range(1, 5):
        backward_step(f, 0)

    for f in range(1, 5):
        def got(which):
            return back_s[pl.ds(f * COLS * 16 + which, 8, stride=16), :]

        dz, dx, dy, inverse, live, slope = (geo_s[f, 8 + which] for which in range(6))
        d_dist = jnp.zeros((8, 128), F32)
        for k in range(NB):
            d_dist = d_dist + got(k) * geo_s[f, k]
        readout = jnp.zeros((8, 128), F32)
        col = iota((8, 128), 0)
        for i in range(1, 5):
            value = hout_s[(f * 4 + i - 1) * 8 : (f * 4 + i - 1) * 8 + 8, :]
            readout = jnp.where(col == ((col0 + (i + COLS - 2)) & (COLS - 1)), value, readout)
        d_dist = d_dist + readout * live * slope
        hz, hx, hy = (got(8 + m) * live for m in (1, 2, 3))
        d_dist = d_dist - (hz * dz + hx * dx + hy * dy) * inverse * inverse
        along = d_dist * inverse
        for axis, (delta, own) in enumerate(((dz, hz), (dx, hx), (dy, hy))):
            value = along * delta + own * inverse
            high = value.astype(BF16).astype(F32)
            vec_s[pl.ds(f * COLS * 8 + 2 * axis, 8, stride=8), :] = high
            vec_s[pl.ds(f * COLS * 8 + 2 * axis + 1, 8, stride=8), :] = value - high
        for spare in (6, 7):
            vec_s[pl.ds(f * COLS * 8 + spare, 8, stride=8), :] = jnp.zeros((8, 128), F32)

    total = [[jnp.zeros((8, 128), F32) for _ in range(2)] for _ in range(2)]
    for f in range(1, 5):
        for i in range(1, 5):
            vec = vec_s[pl.ds(slot(f, i) * 8, 8), :]
            place = bin_rows(f, i, 28, 1)
            targets = [(dr, dc) for dr in (-1, 0, 1) for dc in (-1, 0, 1) if 2 <= i + dc <= 3 and 2 <= f + dr <= 3]
            parts = [vec * flag(place == float((dr + 1) * 3 + dc + 1)) for dr, dc in targets]
            if len(parts) % 2:
                parts.append(jnp.zeros((8, 128), F32))
            moved = dot(jnp.concatenate(parts, axis=0).astype(BF16), hot_a_s[f, i - 1])
            for index, (dr, dc) in enumerate(targets):
                total[f + dr - 2][i + dc - 2] -= moved[8 * index : 8 * index + 8]
            if i in (2, 3) and f in (2, 3):
                centered = jnp.concatenate([vec, jnp.zeros((8, 128), F32)], axis=0).astype(BF16)
                total[f - 2][i - 2] += dot(centered, hot_c_s[f, i - 1])[0:8]
    for row in range(2):
        for col in range(2):
            value = total[row][col]
            for axis in range(3):
                force_ref[axis, row, pl.ds(col, 1), :] = (
                    value[2 * axis : 2 * axis + 1] + value[2 * axis + 1 : 2 * axis + 2]
                )


FEATURE_GROUPS = ((0, 1, 2, 3, 4, 5),)
ENERGY_GROUPS = ((0, 5), (1, 2, 3, 4))
RIM_GROUPS = ((0, 1, 2, 3, 4, 5),)
BACK_GROUPS = ((1, 2, 3, 4),)


def compute(far, mid, near, in_weight, env_weight, up_weight, out_weight):
    return pl.pallas_call(
        kernel,
        out_shape=(
            jax.ShapeDtypeStruct((2, 2, 128), F32),
            jax.ShapeDtypeStruct((3, 2, 2, 128), F32),
        ),
        in_specs=[pl.BlockSpec(memory_space=pltpu.VMEM)] * 7,
        out_specs=[pl.BlockSpec(memory_space=pltpu.VMEM)] * 2,
        scratch_shapes=[
            pltpu.VMEM((12 * COLS * 8, 128), F32),
            pltpu.VMEM((6 * COLS * 32, 128), F32),
            pltpu.VMEM((6, 16, COLS, 128), F32),
            pltpu.VMEM((80, 768), BF16),
            pltpu.VMEM((256, 256), BF16),
            pltpu.VMEM((256, 256), BF16),
            pltpu.VMEM((512, 256), BF16),
            pltpu.VMEM((256, 512), BF16),
            pltpu.VMEM((32, 512), BF16),
            pltpu.VMEM((16, 256), BF16),
            pltpu.VMEM((6, 6, 128, 256), BF16),
            pltpu.VMEM((6, 4, 128, 128), F32),
            pltpu.VMEM((6, 4, 128, 128), F32),
            pltpu.VMEM((6, 4, 128, 128), F32),
            pltpu.VMEM((6, 6, 128, 128), BF16),
            pltpu.VMEM((8, 128), F32),
            pltpu.VMEM((6, 4, 128, 128), F32),
            pltpu.VMEM((6 * 4 * 8, 128), F32),
            pltpu.VMEM((6 * COLS * 16, 128), F32),
            pltpu.VMEM((6 * COLS * 8, 128), F32),
            pltpu.VMEM((6, 4, 128, 256), BF16),
            pltpu.VMEM((6, 6, 128, 256), BF16),
            pltpu.VMEM((6, 4, 128, 128), BF16),
            pltpu.VMEM((6, 4, 128, 128), BF16),
            pltpu.VMEM((6, 6, 128, 128), BF16),
            pltpu.VMEM((6, 6, 128, 384), BF16),
            pltpu.VMEM((6, 6, 128, 128), F32),
        ],
        compiler_params=pltpu.CompilerParams(vmem_limit_bytes=40 * 1024 * 1024),
        name="potential",
    )(far, mid, near, in_weight, env_weight, up_weight, out_weight)


def pack_kernel(coords_ref, species_ref, centers_ref, others_ref, live_ref, packed_ref):
    for row in range(2):
        for col in range(2):
            at = pl.ds(col, 1)
            tile = jnp.concatenate(
                [coords_ref[axis, row, at, :] for axis in range(3)]
                + [ref[row, at, :].astype(F32) for ref in (species_ref, centers_ref, others_ref)]
                + [jnp.full((1, 128), live_ref[row, col], jnp.int32).astype(F32), jnp.zeros((1, 128), F32)],
                axis=0,
            )
            for peer in range(8):
                packed_ref[peer, row, col] = tile


def pack(coords, species, centers, others, live_count):
    return pl.pallas_call(
        pack_kernel,
        out_shape=jax.ShapeDtypeStruct((8, 2, 2, 8, 128), F32),
        in_specs=[pl.BlockSpec(memory_space=pltpu.VMEM)] * 4 + [pl.BlockSpec(memory_space=pltpu.SMEM)],
        out_specs=pl.BlockSpec(memory_space=pltpu.VMEM),
        name="pack",
    )(coords, species, centers, others, live_count)


def swap(value, count, first):
    return lax.ppermute(value, "gz", [(i, (((i + first) ^ 2) - first) % count) for i in range(count)])


def body(
    coords, species, centers, others, live_count, in_weight, env_weight, up_weight, out_weight
):
    packed = pack(coords, species, centers, others, live_count)
    depth, width = lax.axis_size("gz"), lax.axis_size("xy")
    chips = [
        [(2 * chip + core) * width + place for core in range(2) for place in range(width)]
        for chip in range(depth // 2)
    ]
    mid = lax.all_to_all(packed, ("gz", "xy"), 0, 0, tiled=True, axis_index_groups=chips)
    near = swap(mid, depth, 0)
    far = swap(mid[..., :7, :], depth, 2)
    return compute(far, mid, near, in_weight, env_weight, up_weight, out_weight.reshape(1, -1))


def solution(mesh):
    in_specs = (
        P(None, "gz", "xy", None),
        P("gz", "xy", None),
        P("gz", "xy", None),
        P("gz", "xy", None),
        P("gz", "xy"),
        P(),
        P(),
        P(),
        P(),
    )
    out_specs = (P("gz", "xy", None), P(None, "gz", "xy", None))
    return jax.shard_map(body, mesh=mesh, in_specs=in_specs, out_specs=out_specs, check_vma=False)
```

```python
import jax
import jax.numpy as jnp
from jax import lax
from jax.experimental import pallas as pl
from jax.experimental.pallas import tpu as pltpu
from jax.sharding import PartitionSpec as P

NB = 8
SPEC = 8
LAT = 128
CH = 32
SOFTEN = 0.01
CUTOFF = 3.5
COLS = 8
F32 = jnp.float32
BF16 = jnp.bfloat16
PI = 3.141592653589793


def halves(value):
    high = value.astype(BF16)
    low = (value - high.astype(F32)).astype(BF16)
    return high, low


def dot(left, right):
    return lax.dot_general(left, right, (((1,), (0,)), ((), ())), preferred_element_type=F32)


def dot_t(left, right):
    return lax.dot_general(left, right, (((1,), (1,)), ((), ())), preferred_element_type=F32)


def t_dot(left, right):
    return lax.dot_general(left, right, (((0,), (0,)), ((), ())), preferred_element_type=F32)


def both(value):
    return value[:, :128] + value[:, 128:]


def iota(shape, dim):
    return lax.broadcasted_iota(jnp.int32, shape, dim)


def flag(condition):
    return jnp.where(condition, 1.0, 0.0).astype(F32)


def kernel(
    low_ref, mid_ref, high_ref, in_ref, env_ref, up_ref, out_ref,
    energy_ref, force_ref,
    grid_s, rows_s, geo_s, w_first, w_env, w_env_t, w_up, w_down, w_rad, w_out,
    lat_s, slope_s, harm_s, msg_s, feat_s, dfeat_s, dlat_s, hout_s, back_s, vec_s,
    dfi_s, dfj_s, hot_c_s, hot_a_s, hot_at_s, index_s, weight_s,
):
    col0 = lax.axis_index("xy") * 2
    first_row = (lax.axis_index("gz") % 2) * 2 + 1

    lane = iota((128, 128), 1)
    sub = iota((128, 128), 0)
    w_in = in_ref[...]
    wr_hi, wr_lo = halves(w_in[0:8])
    wi_hi, wi_lo = halves(w_in[8:16])
    wj_hi, wj_lo = halves(w_in[16:24])
    lane8 = iota((8, 128), 1)
    sub8 = iota((8, 128), 0)
    spread = flag((lane8 // CH) == (sub8 % 4))
    first = jnp.concatenate(
        [x.astype(F32) for x in (wr_hi, wr_hi, wr_lo, wi_hi, wi_lo, wj_hi, wj_lo)], axis=0
    )
    w_first[:, 0:128] = jnp.concatenate([first, jnp.zeros((24, 128), F32)], axis=0).astype(BF16)
    w_first[:, 128:256] = jnp.concatenate(
        [jnp.zeros((56, 128), F32), spread, jnp.zeros((16, 128), F32)], axis=0
    ).astype(BF16)
    for block, table in enumerate(
        (
            flag(sub8 == 2),
            flag(sub8 == 3),
            flag(sub8 == 4),
            flag((sub8 == 5) | (sub8 == 6)),
        )
    ):
        w_first[:, 128 * block + 256 : 128 * block + 384] = jnp.concatenate(
            [jnp.zeros((64, 128), F32), table, jnp.zeros((8, 128), F32)], axis=0
        ).astype(BF16)
    env = env_ref[...]
    env_hi, env_lo = halves(env)
    tile = flag((iota((CH, 128), 1) % CH) == iota((CH, 128), 0)).astype(BF16)
    env4_hi = dot(env_hi, tile)
    env4_lo = dot(env_lo, tile)
    zero = jnp.zeros((128, 128), BF16)
    w_env[0:128, 0:128] = env4_hi.astype(BF16)
    w_env[0:128, 128:256] = env4_lo.astype(BF16)
    w_env[128:256, 0:128] = env4_hi.astype(BF16)
    w_env[128:256, 128:256] = zero
    env4_hi_t = jnp.transpose(env4_hi).astype(BF16)
    env4_lo_t = jnp.transpose(env4_lo).astype(BF16)
    w_env_t[0:128, 0:128] = env4_hi_t
    w_env_t[0:128, 128:256] = env4_lo_t
    w_env_t[128:256, 0:128] = env4_hi_t
    w_env_t[128:256, 128:256] = zero
    up = up_ref[...]
    up_l = up[0:128]
    up_p = jnp.concatenate([up[128:160]] * 4, axis=0)
    for base, block in ((0, up_l), (256, up_p)):
        hi, lo = halves(block)
        w_up[base : base + 128, 0:128] = hi
        w_up[base : base + 128, 128:256] = lo
        w_up[base + 128 : base + 256, 0:128] = hi
        w_up[base + 128 : base + 256, 128:256] = zero
        hi, lo = halves(jnp.transpose(block))
        w_down[0:128, base : base + 128] = hi
        w_down[128:256, base : base + 128] = hi
        w_down[0:128, base + 128 : base + 256] = lo
        w_down[128:256, base + 128 : base + 256] = zero
    z8 = jnp.zeros((8, 128), F32)
    wr_hi32 = wr_hi.astype(F32)
    wr_lo32 = wr_lo.astype(F32)
    ones4 = flag((lane8 // CH) == sub8)
    for block, parts in enumerate(
        ((wr_hi32, wr_lo32, z8, z8), (wr_hi32, z8, z8, z8), (z8, z8, ones4, z8), (z8, z8, ones4, z8))
    ):
        w_rad[:, 128 * block : 128 * block + 128] = jnp.concatenate(parts, axis=0).astype(BF16)
    out_row = out_ref[...]
    out_hi, out_lo = halves(out_row)
    out_hi32 = out_hi.astype(F32)
    out_lo32 = out_lo.astype(F32)
    z1 = jnp.zeros((1, 128), F32)
    pad14 = jnp.zeros((14, 128), F32)
    w_out[:, 0:128] = jnp.concatenate([out_hi32, out_lo32, pad14], axis=0).astype(BF16)
    w_out[:, 128:256] = jnp.concatenate([out_hi32, z1, pad14], axis=0).astype(BF16)

    for source, start in ((low_ref, 0), (mid_ref, 4), (high_ref, 8)):
        for peer in range(8):
            for row in range(2):
                for col in range(2):
                    place = ((start + peer // 4 * 2 + row) * COLS + peer % 4 * 2 + col) * 8
                    size = source.shape[3]
                    grid_s[place : place + size, :] = source[peer, row, col]

    def quantity(row, which):
        return grid_s[pl.ds((first_row + row) * 64 + which, 8, stride=8), :]

    tables = [[quantity(row, which) for which in range(4)] for row in range(8)]
    for f in range(6):
        center = quantity(f + 1, 4)
        other = quantity(f + 1, 5)
        count = quantity(f + 1, 6)
        center_i = center.astype(jnp.int32)
        other_i = other.astype(jnp.int32)
        place = other_i // 128
        atom = other_i % 128
        at_i = [jnp.take_along_axis(tables[f + 1][which], center_i, axis=1) for which in range(4)]
        at_j = [jnp.zeros((8, 128), F32) for _ in range(4)]
        for offset in range(9):
            dr, dc = offset // 3 - 1, offset % 3 - 1
            here = place == offset
            for which in range(4):
                table = tables[f + 1 + dr][which]
                if dc:
                    table = pltpu.roll(table, (-dc) % 8, 0)
                value = jnp.take_along_axis(table, atom, axis=1)
                if which == 0:
                    value = value + float(dr)
                if which == 1:
                    value = value + float(dc)
                at_j[which] = jnp.where(here, value, at_j[which])
        dz, dx, dy = (at_j[which] - at_i[which] for which in range(3))
        distance = jnp.sqrt(dz * dz + dx * dx + dy * dy + SOFTEN)
        inverse = 1.0 / distance
        scaled = distance * (1.0 / CUTOFF)
        inner = 1.0 - scaled * scaled
        envelope = inner * inner
        slope = (-4.0 / CUTOFF) * inner * scaled
        live = flag(iota((8, 128), 1).astype(F32) < count)
        angle = PI * scaled
        sine, cosine = jnp.sin(angle), jnp.cos(angle)
        base = f * COLS * 32

        def put(which, value):
            rows_s[pl.ds(base + which, 8, stride=32), :] = value

        def split_put(which, gap, value):
            high = value.astype(BF16).astype(F32)
            put(which, high)
            put(which + gap, value - high)

        s_old, s_now = jnp.zeros_like(sine), sine
        c_old, c_now = jnp.ones_like(sine), cosine
        scale = inverse * envelope
        slope_scale = inverse * slope - inverse * scale
        for k in range(1, NB + 1):
            split_put(k - 1, 8, s_now * scale)
            geo_s[f, k - 1] = (k * PI / CUTOFF) * c_now * scale + s_now * slope_scale
            s_old, s_now = s_now, 2.0 * cosine * s_now - s_old
            c_old, c_now = c_now, 2.0 * cosine * c_now - c_old
        for m, value in enumerate((live, live * dz * inverse, live * dx * inverse, live * dy * inverse)):
            split_put(16 + m, 4, value)
        put(24, at_i[3])
        put(25, at_j[3])
        put(26, center)
        put(27, atom.astype(F32))
        put(28, place.astype(F32))
        split_put(29, 1, envelope * live)
        put(31, live)
        for which, value in enumerate((dz, dx, dy, inverse, live, slope, envelope)):
            geo_s[f, 8 + which] = value

    def slot(f, i):
        return f * COLS + ((col0 + (i + COLS - 2)) & (COLS - 1))

    def bin_rows(f, i, first, size):
        return rows_s[pl.ds(slot(f, i) * 32 + first, size), :]

    lanes = iota((128, 128), 1).astype(F32).astype(BF16)
    subs = iota((128, 128), 0).astype(F32).astype(BF16)
    one = jnp.ones((128, 128), BF16)

    def hot_rows(row):
        wide = jnp.broadcast_to(row, (128, 128)).astype(BF16)
        return jnp.where(wide == subs, one, zero)

    def feature_group(f, cols):
        inputs = []
        for i in cols:
            rows = bin_rows(f, i, 0, 32)
            spec_i = flag(rows[24:25] == iota((8, 128), 0).astype(F32))
            spec_j = flag(rows[25:26] == iota((8, 128), 0).astype(F32))
            inputs.append(jnp.concatenate(
                [rows[0:16], rows[0:8], spec_i, spec_i, spec_j, spec_j, rows[16:32], jnp.zeros((8, 128), F32)],
                axis=0,
            ).astype(BF16))
        mixed = t_dot(jnp.concatenate(inputs, axis=1), w_first[...])
        pre, harm = mixed[:, :128], mixed[:, 128:256]
        narrow = mixed[:, 256:640].astype(BF16)
        gate = 0.5 + 0.5 * jnp.tanh(0.5 * pre)
        latent = pre * gate
        lat = jnp.concatenate(halves(latent), axis=1)
        weights = both(dot(lat, w_env[...]))
        slope = gate + latent * (1.0 - gate)
        high, low = halves(weights * harm)
        for n, i in enumerate(cols):
            part = slice(128 * n, 128 * n + 128)
            message = jnp.concatenate([high[part], low[part]], axis=0)
            hot = hot_rows(bin_rows(f, i, 26, 1))
            feat = dot(jnp.concatenate([hot, hot], axis=1), message)
            lat_s[f, i] = lat[part]
            index_s[f, i] = narrow[part]
            weight_s[f, i] = mixed[part, 640:]
            feat_s[f, i] = feat.astype(BF16)
            if 1 <= i <= 4:
                slope_s[f, i - 1] = slope[part]
                harm_s[f, i - 1] = harm[part]
                msg_s[f, i - 1] = weights[part]

    def feature_step(f, carry):
        for group in FEATURE_GROUPS:
            feature_group(f, group)
        return carry

    for f in range(6):
        feature_step(f, 0)

    def energy_group(f, cols, reach, inside_row):
        feat_i, feat_j, weight, hots = [], [], [], []
        for i in cols:
            inside = inside_row and 1 <= i <= 4
            narrow = index_s[f, i]
            center, atom, place = narrow[:, :128], narrow[:, 128:256], narrow[:, 256:]
            weight.append(weight_s[f, i])
            hot_c = jnp.where(center == lanes, one, zero)
            hot_a = jnp.where(atom == lanes, one, zero)
            feat_i.append(dot(hot_c, feat_s[f, i]))
            columns, tables_j = [], []
            for target, code in reach:
                for dc in (-1, 0, 1):
                    if inside or 1 <= i + dc <= 4:
                        columns.append(jnp.where(place == jnp.asarray(code + (dc + 1), F32).astype(BF16), hot_a, zero))
                        tables_j.append(feat_s[target, i + dc])
            feat_j.append(dot(jnp.concatenate(columns, axis=1), jnp.concatenate(tables_j, axis=0)))
            hots.append(hot_c)
            if inside:
                hot_c_s[f, i - 1] = hot_c
                hot_a_s[f, i - 1] = hot_a
            hot_at_s[f, i] = hot_rows(bin_rows(f, i, 27, 1))
        feat_i = jnp.concatenate(feat_i, axis=0)
        feat_j = jnp.concatenate(feat_j, axis=0)
        weight = jnp.concatenate(weight, axis=0)
        lat = jnp.concatenate([lat_s[f, i] for i in cols], axis=0)
        prod = jnp.concatenate(halves(feat_i * feat_j), axis=1)
        pre = both(dot(jnp.concatenate([lat, prod], axis=1), w_up[...]))
        gate = 0.5 + 0.5 * jnp.tanh(0.5 * pre)
        hidden = pre * gate
        d_pre = out_ref[...] * (gate + hidden * (1.0 - gate)) * weight
        d_pre = jnp.concatenate(halves(d_pre), axis=1)
        within = inside_row and 1 <= cols[0] <= 4
        if within:
            down = dot(d_pre, w_down[...])
            d_lat = both(down[:, :256])
            d_prod = both(down[:, 256:])
            hid = jnp.concatenate(halves(hidden), axis=1)
            readout = dot_t(w_out[...], hid)
            d_i = jnp.concatenate(halves(d_prod * feat_j), axis=1)
        else:
            d_prod = both(dot(d_pre, w_down[:, 256:]))
        d_j = jnp.concatenate(halves(d_prod * feat_i), axis=1)
        for n, i in enumerate(cols):
            part = slice(128 * n, 128 * n + 128)
            dfj_s[f, i] = d_j[part]
            if within:
                dfi_s[f, i - 1] = d_i[part]
                dlat_s[f, i - 1] = d_lat[part]
                value = readout[0:1, part] + readout[1:2, part]
                hout_s[pl.ds((f * 4 + (i - 1)) * 8, 8), :] = jnp.broadcast_to(value, (8, 128))
                if i in (2, 3):
                    rows = bin_rows(f, i, 24, 8)
                    edge = value * (rows[5:6] + rows[6:7])
                    high = edge.astype(BF16).astype(F32)
                    parts = jnp.concatenate([high, edge - high, jnp.zeros((14, 128), F32)], axis=0)
                    summed = dot(parts.astype(BF16), hots[n])
                    energy_ref[jnp.clip(f - 2, 0, 1), pl.ds(i - 2, 1), :] = jnp.where(
                        (f == 2) | (f == 3), summed[0:1] + summed[1:2],
                        energy_ref[jnp.clip(f - 2, 0, 1), pl.ds(i - 2, 1), :])

    def energy_step(f, carry):
        reach = [(f + dr, 3.0 * (dr + 1)) for dr in (-1, 0, 1)]
        for group in ENERGY_GROUPS:
            energy_group(f, group, reach, True)
        return carry

    def rim_step(t, carry):
        for group in RIM_GROUPS:
            energy_group(5 * t, group, [(1 + 3 * t, 6.0 - 6.0 * t.astype(F32))], False)
        return carry

    energy_ref[...] = jnp.zeros_like(energy_ref)
    for f in range(1, 5):
        energy_step(f, 0)
    lax.fori_loop(0, 2, rim_step, 0)

    def backward_group(f, cols):
        d_msg = []
        for i in cols:
            columns, terms = [hot_rows(bin_rows(f, i, 26, 1))], [dfi_s[f, i - 1]]
            for dr in (-1, 0, 1):
                for dc in (-1, 0, 1):
                    code = float(3 * (1 - dr) + (1 - dc))
                    mask = flag(bin_rows(f + dr, i + dc, 28, 1) == code)
                    mask = jnp.broadcast_to(mask, (128, 128)).astype(BF16)
                    columns.append(hot_at_s[f + dr, i + dc] * mask)
                    terms.append(dfj_s[f + dr, i + dc])
            d_feat = both(dot(jnp.concatenate(columns, axis=1), jnp.concatenate(terms, axis=0)))
            hot = hot_c_s[f, i - 1]
            d_msg.append(dot(jnp.concatenate([hot, hot], axis=1), jnp.concatenate(halves(d_feat), axis=0)))
        d_msg = jnp.concatenate(d_msg, axis=0)
        gather = lambda ref: jnp.concatenate([ref[f, i - 1] for i in cols], axis=0)
        d_weight = jnp.concatenate(halves(d_msg * gather(harm_s)), axis=1)
        d_lat = both(dot(d_weight, w_env_t[...])) + gather(dlat_s)
        d_pre = jnp.concatenate(
            halves(d_lat * gather(slope_s)) + halves(d_msg * gather(msg_s)), axis=1
        )
        rows = dot_t(w_rad[...], d_pre)
        result = jnp.concatenate([rows[0:8] + rows[8:16], rows[16:24]], axis=0)
        for n, i in enumerate(cols):
            back_s[pl.ds(slot(f, i) * 16, 16), :] = result[:, 128 * n : 128 * n + 128]

    def backward_step(f, carry):
        for group in BACK_GROUPS:
            backward_group(f, group)
        return carry

    back_s[...] = jnp.zeros_like(back_s)
    for f in range(1, 5):
        backward_step(f, 0)

    for f in range(1, 5):
        def got(which):
            return back_s[pl.ds(f * COLS * 16 + which, 8, stride=16), :]

        dz, dx, dy, inverse, live, slope = (geo_s[f, 8 + which] for which in range(6))
        d_dist = jnp.zeros((8, 128), F32)
        for k in range(NB):
            d_dist = d_dist + got(k) * geo_s[f, k]
        readout = jnp.zeros((8, 128), F32)
        col = iota((8, 128), 0)
        for i in range(1, 5):
            value = hout_s[(f * 4 + i - 1) * 8 : (f * 4 + i - 1) * 8 + 8, :]
            readout = jnp.where(col == ((col0 + (i + COLS - 2)) & (COLS - 1)), value, readout)
        d_dist = d_dist + readout * live * slope
        hz, hx, hy = (got(8 + m) * live for m in (1, 2, 3))
        d_dist = d_dist - (hz * dz + hx * dx + hy * dy) * inverse * inverse
        along = d_dist * inverse
        for axis, (delta, own) in enumerate(((dz, hz), (dx, hx), (dy, hy))):
            value = along * delta + own * inverse
            high = value.astype(BF16).astype(F32)
            vec_s[pl.ds(f * COLS * 8 + 2 * axis, 8, stride=8), :] = high
            vec_s[pl.ds(f * COLS * 8 + 2 * axis + 1, 8, stride=8), :] = value - high
        for spare in (6, 7):
            vec_s[pl.ds(f * COLS * 8 + spare, 8, stride=8), :] = jnp.zeros((8, 128), F32)

    total = [[jnp.zeros((8, 128), F32) for _ in range(2)] for _ in range(2)]
    for f in range(1, 5):
        for i in range(1, 5):
            vec = vec_s[pl.ds(slot(f, i) * 8, 8), :]
            place = bin_rows(f, i, 28, 1)
            targets = [(dr, dc) for dr in (-1, 0, 1) for dc in (-1, 0, 1) if 2 <= i + dc <= 3 and 2 <= f + dr <= 3]
            parts = [vec * flag(place == float((dr + 1) * 3 + dc + 1)) for dr, dc in targets]
            if len(parts) % 2:
                parts.append(jnp.zeros((8, 128), F32))
            moved = dot(jnp.concatenate(parts, axis=0).astype(BF16), hot_a_s[f, i - 1])
            for index, (dr, dc) in enumerate(targets):
                total[f + dr - 2][i + dc - 2] -= moved[8 * index : 8 * index + 8]
            if i in (2, 3) and f in (2, 3):
                centered = jnp.concatenate([vec, jnp.zeros((8, 128), F32)], axis=0).astype(BF16)
                total[f - 2][i - 2] += dot(centered, hot_c_s[f, i - 1])[0:8]
    for row in range(2):
        for col in range(2):
            value = total[row][col]
            for axis in range(3):
                force_ref[axis, row, pl.ds(col, 1), :] = (
                    value[2 * axis : 2 * axis + 1] + value[2 * axis + 1 : 2 * axis + 2]
                )


FEATURE_GROUPS = ((0, 1, 2, 3, 4, 5),)
ENERGY_GROUPS = ((0, 5), (1, 2, 3, 4))
RIM_GROUPS = ((0, 1, 2, 3, 4, 5),)
BACK_GROUPS = ((1, 2, 3, 4),)


def compute(low, mid, high, in_weight, env_weight, up_weight, out_weight):
    return pl.pallas_call(
        kernel,
        out_shape=(
            jax.ShapeDtypeStruct((2, 2, 128), F32),
            jax.ShapeDtypeStruct((3, 2, 2, 128), F32),
        ),
        in_specs=[pl.BlockSpec(memory_space=pltpu.VMEM)] * 7,
        out_specs=[pl.BlockSpec(memory_space=pltpu.VMEM)] * 2,
        scratch_shapes=[
            pltpu.VMEM((12 * COLS * 8, 128), F32),
            pltpu.VMEM((6 * COLS * 32, 128), F32),
            pltpu.VMEM((6, 16, COLS, 128), F32),
            pltpu.VMEM((80, 768), BF16),
            pltpu.VMEM((256, 256), BF16),
            pltpu.VMEM((256, 256), BF16),
            pltpu.VMEM((512, 256), BF16),
            pltpu.VMEM((256, 512), BF16),
            pltpu.VMEM((32, 512), BF16),
            pltpu.VMEM((16, 256), BF16),
            pltpu.VMEM((6, 6, 128, 256), BF16),
            pltpu.VMEM((6, 4, 128, 128), F32),
            pltpu.VMEM((6, 4, 128, 128), F32),
            pltpu.VMEM((6, 4, 128, 128), F32),
            pltpu.VMEM((6, 6, 128, 128), BF16),
            pltpu.VMEM((8, 128), F32),
            pltpu.VMEM((6, 4, 128, 128), F32),
            pltpu.VMEM((6 * 4 * 8, 128), F32),
            pltpu.VMEM((6 * COLS * 16, 128), F32),
            pltpu.VMEM((6 * COLS * 8, 128), F32),
            pltpu.VMEM((6, 4, 128, 256), BF16),
            pltpu.VMEM((6, 6, 128, 256), BF16),
            pltpu.VMEM((6, 4, 128, 128), BF16),
            pltpu.VMEM((6, 4, 128, 128), BF16),
            pltpu.VMEM((6, 6, 128, 128), BF16),
            pltpu.VMEM((6, 6, 128, 384), BF16),
            pltpu.VMEM((6, 6, 128, 128), F32),
        ],
        compiler_params=pltpu.CompilerParams(vmem_limit_bytes=40 * 1024 * 1024),
        name="potential",
    )(low, mid, high, in_weight, env_weight, up_weight, out_weight)


def pack_kernel(coords_ref, species_ref, centers_ref, others_ref, live_ref, packed_ref):
    for row in range(2):
        for col in range(2):
            at = pl.ds(col, 1)
            tile = jnp.concatenate(
                [coords_ref[axis, row, at, :] for axis in range(3)]
                + [ref[row, at, :].astype(F32) for ref in (species_ref, centers_ref, others_ref)]
                + [jnp.full((1, 128), live_ref[row, col], jnp.int32).astype(F32), jnp.zeros((1, 128), F32)],
                axis=0,
            )
            for peer in range(8):
                packed_ref[peer, row, col] = tile


def pack(coords, species, centers, others, live_count):
    return pl.pallas_call(
        pack_kernel,
        out_shape=jax.ShapeDtypeStruct((8, 2, 2, 8, 128), F32),
        in_specs=[pl.BlockSpec(memory_space=pltpu.VMEM)] * 4 + [pl.BlockSpec(memory_space=pltpu.SMEM)],
        out_specs=pl.BlockSpec(memory_space=pltpu.VMEM),
        name="pack",
    )(coords, species, centers, others, live_count)


def shift(value, axis, step):
    count = lax.axis_size(axis)
    return lax.ppermute(value, axis, [(i, (i + step) % count) for i in range(count)])


def body(
    coords, species, centers, others, live_count, in_weight, env_weight, up_weight, out_weight
):
    packed = pack(coords, species, centers, others, live_count)
    depth, width = lax.axis_size("gz"), lax.axis_size("xy")
    chips = [
        [(2 * chip + core) * width + place for core in range(2) for place in range(width)]
        for chip in range(depth // 2)
    ]
    mid = lax.all_to_all(packed, ("gz", "xy"), 0, 0, tiled=True, axis_index_groups=chips)
    low = shift(mid, "gz", 2)
    high = shift(mid[..., :7, :], "gz", -2)
    return compute(low, mid, high, in_weight, env_weight, up_weight, out_weight.reshape(1, -1))


def solution(mesh):
    in_specs = (
        P(None, "gz", "xy", None),
        P("gz", "xy", None),
        P("gz", "xy", None),
        P("gz", "xy", None),
        P("gz", "xy"),
        P(),
        P(),
        P(),
        P(),
    )
    out_specs = (P("gz", "xy", None), P(None, "gz", "xy", None))
    return jax.shard_map(body, mesh=mesh, in_specs=in_specs, out_specs=out_specs, check_vma=False)
```
